512 devices in a mesh: blk: 32 (over z_hi, x, core), lane: 16 (over z_lo, y).
Axes of the slice: x: 4, y: 8, z: 8 (z_hi: 4, z_lo: 2; z = z_hi * 2 + z_lo), core: 2. Of those that a mesh axis runs over, the one named last changes fastest.
Arguments:
- image_feat: bfloat16 [196608, 768], P(('blk', 'lane')), may hold values from -1 to 1
- text_emb: bfloat16 [196608, 768], P(('blk', 'lane')), may hold values from -1 to 1
- head_weight: bfloat16 [768, 768], replicated, may hold values from -0.21875 to 0.21875
- lang_ids: int32 [196608], P(('blk', 'lane')), may hold values from 0 to 108, never falling along the last dimension, each value on 1 to 7214 neighbouring positions
- pair_mask: int32 [109, 109], replicated, may hold values 0 or 1
- weight_codes: int32 [109], replicated, may hold values from 1 to 4
- log_scale: float32 [], replicated, may hold values from 0.693 to 2.079
- logit_bias: float32 [], replicated, may hold values from -3 to -1
Outputs:
- image_back: bfloat16 [196608, 768], P(('blk', 'lane'))
- text_back: bfloat16 [196608, 768], P(('blk', 'lane'))
- head_grad: float32 [768, 768], P('lane', 'blk')
The draws below stay inside these ranges and needn't reach their ends.
Inputs may be any that keep to these rules, and one draw needn't show every extreme that they name: lang_ids never decreases along the rows.
All inputs are finite; a program needn't handle non-finite values.
Results may differ from the reference program's by a relative error of at most 0.022.
Values may be sent and summed in bfloat16 or wider, within the bound.
No kernel may reach another device: no remote copies, remote signals or barrier semaphores. Data moves between devices by JAX's collectives and lax.ppermute only.
A program may use at most 64 MiB of HBM per device.

```python
import math
import jax
import jax.numpy as jnp
import numpy as np
from jax import lax

D = 768
LANGS = 109
ROWS = 384
STEPS = 4
PAIRS = 196608
N_BLK = 32
N_LANE = 16


def draw_image_feat(key, part):
    key = jax.random.fold_in(key, 11)
    keys = jax.random.split(key, 3)
    row_scale = jnp.exp(jax.random.uniform(keys[1], (PAIRS, 1), jnp.float32, 0.0, math.log(10.0)))
    col_scale = jnp.exp(jax.random.uniform(keys[2], (1, D), jnp.float32, 0.0, math.log(10.0)))
    core = jax.random.normal(keys[0], (PAIRS, D), jnp.float32)
    core = jnp.clip(core, -4.0, 4.0)
    return (0.0025 * core * row_scale * col_scale).astype(jnp.bfloat16)


def draw_text_emb(key, part):
    key = jax.random.fold_in(key, 23)
    keys = jax.random.split(key, 3)
    row_scale = jnp.exp(jax.random.uniform(keys[1], (PAIRS, 1), jnp.float32, 0.0, math.log(10.0)))
    col_scale = jnp.exp(jax.random.uniform(keys[2], (1, D), jnp.float32, 0.0, math.log(10.0)))
    core = jax.random.normal(keys[0], (PAIRS, D), jnp.float32)
    core = jnp.clip(core, -4.0, 4.0)
    return (0.0025 * core * row_scale * col_scale).astype(jnp.bfloat16)


def touch_ends(values, key, smallest, top_value):
    spot = [jax.random.randint(jax.random.fold_in(key, axis), (), 0, length) for axis, length in enumerate(values.shape)]
    longest = values.shape.index(max(values.shape))
    beside = spot[:longest] + [(spot[longest] + 1) % values.shape[longest]] + spot[longest + 1:]
    return values.at[tuple(spot)].set(smallest).at[tuple(beside)].set(top_value)


def length_profile(amount, total, limit, lean):
    loads = [(1 << 20) // math.isqrt(rank ** lean) + 1 for rank in range(2, amount + 1)]
    rest, counts = total - limit - (amount - 1), [1] * (amount - 1)
    while rest > 0:
        movable = [i for i in range(amount - 1) if counts[i] < limit]
        whole, left = sum([loads[i] for i in movable]), rest
        for i in movable:
            addition = min(limit - counts[i], max(1, left * loads[i] // whole), rest)
            counts[i] = counts[i] + addition
            rest = rest - addition
    return np.array([limit] + counts)


def uneven(own_key, number_of, total, most, slope):
    if number_of == 2:
        one = jax.random.randint(own_key, (), max(1, total - most), min(most, total - 1) + 1)
        return jnp.stack([one, total - one])
    tallies = jnp.asarray(length_profile(number_of, total, most, slope), jnp.int32)
    pairs = (number_of - 1) // 2
    donor, sink = tallies[1:1 + 2 * pairs:2], tallies[2:2 + 2 * pairs:2]
    room = jnp.minimum(donor - 1, most - sink)
    moved = jax.random.randint(jax.random.fold_in(own_key, 1), (pairs,), 0, 1 << 20) % (room + 1)
    tallies = tallies.at[1:1 + 2 * pairs:2].set(donor - moved).at[2:2 + 2 * pairs:2].set(sink + moved)
    return tallies[jax.random.permutation(jax.random.fold_in(own_key, 2), number_of)]


def centred(stream_key, shape, scale, reach, kind=jnp.bfloat16):
    return jnp.clip(scale * jax.random.normal(stream_key, shape, jnp.float32), -reach, reach).astype(kind)


def setup_inputs(seed: int = 0) -> dict:
    key_of = jax.random.split(jax.random.key(seed), 9)
    image_feat = draw_image_feat(jax.random.fold_in(key_of[8], 71), 0)
    text_emb = draw_text_emb(jax.random.fold_in(key_of[8], 71), 0)
    head_weight = centred(key_of[2], (D, D), D ** -0.5, 0.21875)
    lang_ids = jnp.searchsorted(jnp.cumsum(uneven(key_of[3], LANGS, PAIRS, 4 * PAIRS // LANGS, 2)), jnp.arange(PAIRS), side="right").astype(jnp.int32)
    pair_mask = touch_ends((jax.random.randint(key_of[4], (LANGS, LANGS), 0, 2) < 1).astype(jnp.int32), jax.random.fold_in(key_of[4], 1), 0, 1)
    weight_codes = touch_ends(jax.random.randint(key_of[5], (LANGS,), 1, 5), jax.random.fold_in(key_of[5], 1), 1, 4).astype(jnp.int32)
    log_scale = jnp.clip(jax.random.uniform(key_of[6], (), jnp.float32, 0.693, 2.079), 0.693, 2.079)
    logit_bias = jnp.clip(jax.random.uniform(key_of[7], (), jnp.float32, -3.0, -1.0), -3.0, -1.0)
    return dict(image_feat=image_feat, text_emb=text_emb, head_weight=head_weight, lang_ids=lang_ids, pair_mask=pair_mask, weight_codes=weight_codes, log_scale=log_scale, logit_bias=logit_bias)


EPSILON = 1e-06

def unit_rows(vectors):
    inverse = lax.rsqrt(lax.optimization_barrier(jnp.sum(vectors * vectors, axis=-1, keepdims=True)) + EPSILON)
    return (vectors * inverse, inverse)

def reference(image_feat, text_emb, head_weight, lang_ids, pair_mask, weight_codes, log_scale, logit_bias):
    logit_scale = jnp.exp(log_scale)
    allowed = jnp.maximum(pair_mask, jnp.eye(LANGS, dtype=jnp.int32)).astype(jnp.float32)
    code_vals = weight_codes.astype(jnp.float32)
    labels = jnp.arange(LANGS, dtype=jnp.int32)
    head_wide = head_weight.astype(jnp.float32)

    def by_lane(values_in):
        shaped = values_in.reshape((N_BLK, N_LANE, ROWS) + values_in.shape[1:])
        return jnp.swapaxes(shaped, 0, 1)

    def one_lane(operands):
        features, text_rows, lang_rows = operands
        feat_wide = features.astype(jnp.float32)
        projected = jnp.einsum('brd,de->bre', feat_wide, head_wide)
        image_unit, image_inv = unit_rows(projected)
        text_unit, text_inv = unit_rows(text_rows.astype(jnp.float32))
        image_low = lax.optimization_barrier(image_unit.astype(jnp.bfloat16)).astype(jnp.float32)
        text_low = lax.optimization_barrier(text_unit.astype(jnp.bfloat16)).astype(jnp.float32)
        lang_hot = (lang_rows[..., None] == labels).astype(jnp.float32)
        row_codes = lax.optimization_barrier(jnp.sum(lang_hot * code_vals, axis=-1))
        allow_rows = jnp.einsum('brl,lm->brm', lang_hot, allowed)
        image_grad = jnp.zeros((N_BLK, ROWS, D), jnp.float32)
        text_grad = jnp.zeros((N_BLK, ROWS, D), jnp.float32)
        for offset in range(STEPS):
            text_turn = jnp.roll(text_low, offset, axis=0)
            hot_turn = jnp.roll(lang_hot, offset, axis=0)
            codes_turn = jnp.roll(row_codes, offset, axis=0)
            keep_mask = jnp.einsum('bil,bjl->bij', allow_rows, hot_turn)
            pair_weight = keep_mask * (0.25 * (row_codes[:, :, None] + codes_turn[:, None, :]))
            cosine = jnp.einsum('bid,bjd->bij', image_low, text_turn)
            excess = jax.nn.sigmoid(logit_scale * cosine + logit_bias)
            if offset == 0:
                excess = excess - jnp.eye(ROWS, dtype=jnp.float32)
            pair_grad = lax.optimization_barrier((pair_weight * excess).astype(jnp.bfloat16)).astype(jnp.float32)
            image_grad = image_grad + logit_scale * jnp.einsum('bij,bjd->bid', pair_grad, text_turn)
            text_term = logit_scale * jnp.einsum('bij,bid->bjd', pair_grad, image_low)
            text_grad = text_grad + jnp.roll(text_term, -offset, axis=0)
        radial = lax.optimization_barrier(jnp.sum(image_unit * image_grad, axis=-1, keepdims=True))
        image_dir = ((image_grad - image_unit * radial) * image_inv).astype(jnp.bfloat16)
        dir_wide = image_dir.astype(jnp.float32)
        image_back = jnp.einsum('bre,de->brd', dir_wide, head_wide).astype(jnp.bfloat16)
        head_part = jnp.einsum('brd,bre->de', feat_wide, dir_wide)
        text_radial = lax.optimization_barrier(jnp.sum(text_unit * text_grad, axis=-1, keepdims=True))
        text_back = ((text_grad - text_unit * text_radial) * text_inv).astype(jnp.bfloat16)
        return (image_back, text_back, head_part)
    image_back, text_back, head_parts = lax.map(one_lane, (by_lane(image_feat), by_lane(text_emb), by_lane(lang_ids)))

    def unlane(values_in):
        return jnp.swapaxes(values_in, 0, 1).reshape((PAIRS, D))
    return (unlane(image_back), unlane(text_back), lax.optimization_barrier(jnp.sum(head_parts, axis=0)))
```

```python
import jax
import jax.numpy as jnp
from jax import lax
from jax.sharding import PartitionSpec as P

D = 768
ROWS = 384
N_BLK = 32
EPSILON = 1e-06


def device_index(z_hi, x, core, z_lo, y):
    return ((z_hi * 4 + x) * 2 + core) * 16 + z_lo * 8 + y


CORE_GROUPS = [
    [device_index(z, x, c, l, y) for c in range(2)]
    for z in range(4)
    for x in range(4)
    for l in range(2)
    for y in range(8)
]
NEAR_GROUPS = [
    [device_index(z, x, c, l, 2 * y_hi + y_lo) for x in range(4) for y_lo in range(2)]
    for z in range(4)
    for c in range(2)
    for l in range(2)
    for y_hi in range(4)
]
FAR_GROUPS = [
    [
        device_index(z, x, c, l, 2 * y_hi + y_lo)
        for z in range(4)
        for l in range(2)
        for y_hi in range(4)
    ]
    for x in range(4)
    for c in range(2)
    for y_lo in range(2)
]


def permute(value, target):
    return lax.ppermute(value, "blk", [(i, target(i) % N_BLK) for i in range(N_BLK)])


def swap_cores(value):
    return permute(value, lambda i: i ^ 1)


def exchange(value, groups):
    return lax.all_to_all(value, ("blk", "lane"), 0, 0, axis_index_groups=groups, tiled=True)


def unit_rows(vectors):
    inverse = lax.rsqrt(jnp.sum(vectors * vectors, axis=-1, keepdims=True) + EPSILON)
    return (vectors * inverse, inverse)


def dot(left, right, dims):
    return lax.dot_general(left, right, (dims, ((), ())), preferred_element_type=jnp.float32)


def column_order():
    new = jnp.arange(D, dtype=jnp.int32)
    core, x, z_hi, rest = new // 384, new // 96 % 4, new // 24 % 4, new % 24
    return z_hi * 192 + x * 48 + core * 24 + rest


def row_order():
    new = jnp.arange(D, dtype=jnp.int32)
    y_lo, z_lo, y_hi, rest = new // 384, new // 192 % 2, new // 48 % 4, new % 48
    return z_lo * 384 + (y_hi * 2 + y_lo) * 48 + rest


def order_matrix(old):
    return (jnp.arange(D, dtype=jnp.int32)[:, None] == old[None, :]).astype(jnp.bfloat16)


def on_device(
    image_feat, text_emb, head_weight, lang_ids, pair_mask, weight_codes, log_scale, logit_bias
):
    lang_count = pair_mask.shape[0]
    labels = jnp.arange(lang_count, dtype=jnp.bfloat16)
    logit_scale = jnp.exp(log_scale)
    allowed = jnp.maximum(pair_mask, jnp.eye(lang_count, dtype=jnp.int32)).astype(jnp.float32)
    codes = weight_codes.astype(jnp.float32)
    table = (allowed * (0.25 * (codes[:, None] + codes[None, :]))).astype(jnp.bfloat16)

    langs = lang_ids.astype(jnp.bfloat16)
    tail = jnp.pad(langs[None, :], ((0, 15), (0, D - ROWS)))

    text_unit, text_inv = unit_rows(text_emb.astype(jnp.float32))
    text_low = text_unit.astype(jnp.bfloat16)
    text_out = jnp.concatenate([text_low, tail], axis=0)
    text_far = permute(text_out, lambda i: i + 2)
    text_mix = permute(text_out, lambda i: i + 1 if i % 2 == 0 else i + 3)

    projected = dot(image_feat, head_weight, ((1,), (0,)))
    image_unit, image_inv = unit_rows(projected)
    image_low = image_unit.astype(jnp.bfloat16)
    image_out = jnp.concatenate([image_low, tail], axis=0)
    image_far = permute(image_out, lambda i: i - 2)
    image_mix = permute(image_out, lambda i: i - 1 if i % 2 == 1 else i - 3)

    text_near = swap_cores(text_far)
    image_near = swap_cores(image_far)

    def hot(lang_row):
        return (lang_row[:, None] == labels[None, :]).astype(jnp.bfloat16)

    own_hot = hot(langs)
    own_rows = dot(own_hot, table, ((1,), (0,))).astype(jnp.bfloat16)

    def pair_grad(image, rows, text, text_hot, positive):
        weight = dot(rows, text_hot, ((1,), (1,)))
        logit = logit_scale * dot(image, text, ((1,), (1,))) + logit_bias
        excess = jax.nn.sigmoid(logit)
        if positive:
            excess = excess - jnp.eye(ROWS, dtype=jnp.float32)
        return (weight * excess).astype(jnp.bfloat16)

    grad = pair_grad(image_low, own_rows, text_low, own_hot, True)
    image_sum = dot(grad, text_low, ((1,), (0,)))
    text_sum = dot(grad, image_low, ((0,), (0,)))
    for block in (text_mix, text_far, text_near):
        text = block[:ROWS]
        grad = pair_grad(image_low, own_rows, text, hot(block[ROWS, :ROWS]), False)
        image_sum = image_sum + dot(grad, text, ((1,), (0,)))

    image_grad = logit_scale * image_sum
    radial = jnp.sum(image_unit * image_grad, axis=-1, keepdims=True)
    image_dir = ((image_grad - image_unit * radial) * image_inv).astype(jnp.bfloat16)

    feat_turned = dot(image_feat, order_matrix(row_order()), ((1,), (0,))).astype(jnp.bfloat16)
    dir_turned = dot(image_dir, order_matrix(column_order()), ((1,), (0,))).astype(jnp.bfloat16)
    head = dot(dir_turned, feat_turned, ((0,), (0,))).astype(jnp.bfloat16)
    head = exchange(head, CORE_GROUPS).reshape(2, 384, D)
    head = jnp.sum(head.astype(jnp.float32), axis=0).astype(jnp.bfloat16)
    head = jnp.swapaxes(head.reshape(4, 96, 2, 384), 1, 2).reshape(768, 384)
    head = exchange(head, NEAR_GROUPS).reshape(8, 96, 384)
    head = jnp.sum(head.astype(jnp.float32), axis=0).astype(jnp.bfloat16)
    head = jnp.swapaxes(head.reshape(4, 24, 8, 48), 1, 2).reshape(32, 24, 48)
    head = exchange(head, FAR_GROUPS)
    head_grad = jnp.sum(head.astype(jnp.float32), axis=0).T

    image_back = dot(image_dir, head_weight, ((1,), (1,))).astype(jnp.bfloat16)
    for block in (image_mix, image_far, image_near):
        image = block[:ROWS]
        rows = dot(hot(block[ROWS, :ROWS]), table, ((1,), (0,))).astype(jnp.bfloat16)
        grad = pair_grad(image, rows, text_low, own_hot, False)
        text_sum = text_sum + dot(grad, image, ((0,), (0,)))
    text_grad = logit_scale * text_sum
    text_radial = jnp.sum(text_unit * text_grad, axis=-1, keepdims=True)
    text_back = ((text_grad - text_unit * text_radial) * text_inv).astype(jnp.bfloat16)
    return (image_back, text_back, head_grad)


def solution(mesh):
    in_specs = (
        P(("blk", "lane"), None),
        P(("blk", "lane"), None),
        P(),
        P(("blk", "lane")),
        P(),
        P(),
        P(),
        P(),
    )
    out_specs = (P(("blk", "lane"), None), P(("blk", "lane"), None), P("lane", "blk"))
    return jax.shard_map(
        on_device, mesh=mesh, in_specs=in_specs, out_specs=out_specs, check_vma=False
    )
```

```python
import jax
import jax.numpy as jnp
from jax import lax
from jax.experimental import pallas as pl
from jax.experimental.pallas import tpu as pltpu
from jax.sharding import PartitionSpec as P

D = 768
HALF = D // 2
ROWS = 384
TAIL = 16
LABELS = 128
N_BLK = 32
EPSILON = 1e-06
VMEM_BYTES = 48 * 1024 * 1024


def device_index(z_hi, x, core, z_lo, y):
    return ((z_hi * 4 + x) * 2 + core) * 16 + z_lo * 8 + y


NEAR_GROUPS = [
    [device_index(z, x, c, l, 2 * y_hi + y_lo) for x in range(4) for y_lo in range(2)]
    for z in range(4)
    for c in range(2)
    for l in range(2)
    for y_hi in range(4)
]
FAR_GROUPS = [
    [
        device_index(z, x, c, l, 2 * y_hi + y_lo)
        for z in range(4)
        for l in range(2)
        for y_hi in range(4)
    ]
    for x in range(4)
    for c in range(2)
    for y_lo in range(2)
]


def permute(value, target):
    pairs = [(i, target(i)) for i in range(N_BLK)]
    return lax.ppermute(value, "blk", [(i, j % N_BLK) for i, j in pairs if j is not None])


def swap_cores(value):
    return permute(value, lambda i: i ^ 1)


def exchange(value, groups):
    return lax.all_to_all(value, ("blk", "lane"), 0, 0, axis_index_groups=groups, tiled=True)


def dot(left, right, dims=((1,), (0,))):
    return lax.dot_general(left, right, (dims, ((), ())), preferred_element_type=jnp.float32)


def call(kernel, outs, args, flops, scalars=0):
    smem = pl.BlockSpec(memory_space=pltpu.SMEM)
    vmem = pl.BlockSpec(memory_space=pltpu.VMEM)
    moved = sum(a.size * a.dtype.itemsize for a in tuple(args) + tuple(outs))
    return pl.pallas_call(
        kernel,
        out_shape=outs,
        in_specs=[smem] * scalars + [vmem] * (len(args) - scalars),
        out_specs=[vmem] * len(outs),
        cost_estimate=pl.CostEstimate(flops=flops, bytes_accessed=moved, transcendentals=0),
        compiler_params=pltpu.CompilerParams(vmem_limit_bytes=VMEM_BYTES),
    )(*args)


def array(shape, dtype):
    return jax.ShapeDtypeStruct(shape, dtype)


def text_kernel(text_ref, tail_ref, out_ref):
    text = text_ref[...].astype(jnp.float32)
    inverse = lax.rsqrt(jnp.sum(text * text, axis=-1, keepdims=True) + EPSILON)
    out_ref[:ROWS, :] = (text * inverse).astype(jnp.bfloat16)
    out_ref[ROWS:, :] = tail_ref[...]


def image_kernel(feat_ref, head_ref, tail_ref, out_ref, unit_ref, inv_ref):
    projected = dot(feat_ref[...], head_ref[...])
    inverse = lax.rsqrt(jnp.sum(projected * projected, axis=-1, keepdims=True) + EPSILON)
    unit = projected * inverse
    unit_ref[...] = unit
    inv_ref[...] = inverse
    out_ref[:ROWS, :] = unit.astype(jnp.bfloat16)
    out_ref[ROWS:, :] = tail_ref[...]


def pair_term(scale, bias, own, own_rows, other_ref, positive):
    other = other_ref[:ROWS, :]
    langs = other_ref[ROWS : ROWS + 1, :ROWS].astype(jnp.int32)
    hot = lax.broadcasted_iota(jnp.int32, (LABELS, ROWS), 0) == langs
    weight = dot(own_rows, hot.astype(jnp.float32).astype(jnp.bfloat16))
    logit = scale * dot(own, other, ((1,), (1,))) + bias
    excess = 0.5 + 0.5 * jnp.tanh(0.5 * logit)
    if positive:
        row = lax.broadcasted_iota(jnp.int32, (ROWS, ROWS), 0)
        column = lax.broadcasted_iota(jnp.int32, (ROWS, ROWS), 1)
        excess = jnp.where(row == column, excess - 1.0, excess)
    return dot((weight * excess).astype(jnp.bfloat16), other)


def first_kernel(scalar_ref, own_ref, rows_ref, same_ref, mix_ref, sum_ref):
    scale, bias = scalar_ref[0], scalar_ref[1]
    own, rows = own_ref[:ROWS, :], rows_ref[...]
    sum_ref[...] = pair_term(scale, bias, own, rows, same_ref, True)
    sum_ref[...] += pair_term(scale, bias, own, rows, mix_ref, False)


def next_kernel(scalar_ref, own_ref, rows_ref, other_ref, before_ref, sum_ref):
    scale, bias = scalar_ref[0], scalar_ref[1]
    term = pair_term(scale, bias, own_ref[:ROWS, :], rows_ref[...], other_ref, False)
    sum_ref[...] = before_ref[...] + term


def image_last_kernel(
    scalar_ref, own_ref, rows_ref, other_ref, before_ref, unit_ref, inv_ref, order_ref,
    dir_ref, keep_ref, send_ref,
):
    scale, bias = scalar_ref[0], scalar_ref[1]
    term = pair_term(scale, bias, own_ref[:ROWS, :], rows_ref[...], other_ref, False)
    grad = scale * (before_ref[...] + term)
    unit = unit_ref[...]
    radial = jnp.sum(unit * grad, axis=-1, keepdims=True)
    direction = ((grad - unit * radial) * inv_ref[...]).astype(jnp.bfloat16)
    dir_ref[...] = direction
    turned = dot(order_ref[...], direction, ((1,), (1,))).astype(jnp.bfloat16)
    keep_ref[...] = turned[:HALF, :]
    send_ref[...] = turned[HALF:, :]


def text_last_kernel(
    scalar_ref, own_ref, rows_ref, other_ref, before_ref, text_ref, out_ref
):
    scale, bias = scalar_ref[0], scalar_ref[1]
    term = pair_term(scale, bias, own_ref[:ROWS, :], rows_ref[...], other_ref, False)
    grad = scale * (before_ref[...] + term)
    text = text_ref[...].astype(jnp.float32)
    inverse = lax.rsqrt(jnp.sum(text * text, axis=-1, keepdims=True) + EPSILON)
    unit = text * inverse
    radial = jnp.sum(unit * grad, axis=-1, keepdims=True)
    out_ref[...] = ((grad - unit * radial) * inverse).astype(jnp.bfloat16)


def head_kernel(keep_ref, feat_ref, got_ref, feat_near_ref, out_ref):
    head = dot(keep_ref[...], feat_ref[...]) + dot(got_ref[...], feat_near_ref[...])
    head = head.astype(jnp.bfloat16)
    for x in range(4):
        for y_lo in range(2):
            out_ref[2 * x + y_lo] = head[96 * x : 96 * x + 96, HALF * y_lo : HALF * y_lo + HALF]


def back_kernel(dir_ref, head_ref, out_ref):
    out_ref[...] = dot(dir_ref[...], head_ref[...], ((1,), (1,))).astype(jnp.bfloat16)


def column_order(core):
    new = jnp.arange(D, dtype=jnp.int32)
    side, x, z_hi, rest = new // 384, new // 96 % 4, new // 24 % 4, new % 24
    return z_hi * 192 + x * 48 + (side ^ core) * 24 + rest


def row_order():
    new = jnp.arange(D, dtype=jnp.int32)
    y_lo, z_lo, y_hi, rest = new // 384, new // 192 % 2, new // 48 % 4, new % 48
    return z_lo * 384 + (y_hi * 2 + y_lo) * 48 + rest


def order_matrix(old):
    return (old[:, None] == jnp.arange(D, dtype=jnp.int32)[None, :]).astype(jnp.bfloat16)


def on_device(
    image_feat, text_emb, head_weight, lang_ids, pair_mask, weight_codes, log_scale, logit_bias
):
    place = lax.axis_index("blk") % 8
    lang_count = pair_mask.shape[0]
    allowed = jnp.maximum(pair_mask, jnp.eye(lang_count, dtype=jnp.int32)).astype(jnp.float32)
    codes = weight_codes.astype(jnp.float32)
    table = (allowed * (0.25 * (codes[:, None] + codes[None, :]))).astype(jnp.bfloat16)
    extra = LABELS - lang_count
    table = jnp.pad(table, ((0, extra), (0, extra)))
    scalars = jnp.stack([jnp.exp(log_scale), logit_bias])
    tail = jnp.pad(lang_ids.astype(jnp.bfloat16)[None, :], ((0, TAIL - 1), (0, D - ROWS)))
    block = array((ROWS + TAIL, D), jnp.bfloat16)
    total = array((ROWS, D), jnp.float32)
    pair_flops = 2 * ROWS * ROWS * (2 * D + LABELS)

    (text_out,) = call(text_kernel, [block], (text_emb, tail), 4 * ROWS * D)
    text_far = permute(text_out, lambda i: i + 2 if i % 8 != 7 else None)
    text_via = permute(text_out, lambda i: i + 8 if i % 8 in (5, 7) else None)
    text_mix = permute(
        text_out, lambda i: i + 1 if i % 2 == 0 else (i + 3 if i % 8 != 5 else None)
    )

    image_out, image_unit, image_inv = call(
        image_kernel,
        [block, total, array((ROWS, 1), jnp.float32)],
        (image_feat, head_weight, tail),
        2 * ROWS * D * D,
    )
    image_far = permute(image_out, lambda i: i - 2 if i % 8 != 0 else None)
    image_via = permute(image_out, lambda i: i - 8 if i % 8 in (0, 2) else None)
    image_mix = permute(
        image_out, lambda i: i - 1 if i % 2 == 1 else (i - 3 if i % 8 != 2 else None)
    )

    own_hot = (lang_ids[:, None] == jnp.arange(LABELS)[None, :]).astype(jnp.bfloat16)
    image_rows = dot(own_hot, table).astype(jnp.bfloat16)
    text_rows = dot(own_hot, table, ((1,), (1,))).astype(jnp.bfloat16)
    feat_turned = dot(image_feat, order_matrix(row_order()), ((1,), (1,))).astype(jnp.bfloat16)
    feat_near = swap_cores(feat_turned)
    order = order_matrix(column_order(place % 2))

    text_hop = permute(text_via, lambda i: {7: i - 6, 5: i - 5}.get(i % 8))
    text_far = jnp.where(place == 1, text_hop, text_far)
    text_mix = jnp.where(place == 0, text_hop, text_mix)
    text_near = swap_cores(text_far)
    image_hop = permute(image_via, lambda i: {0: i + 6, 2: i + 5}.get(i % 8))
    image_far = jnp.where(place == 6, image_hop, image_far)
    image_mix = jnp.where(place == 7, image_hop, image_mix)
    image_near = swap_cores(image_far)

    (image_sum,) = call(
        first_kernel,
        [total],
        (scalars, image_out, image_rows, text_out, text_mix),
        2 * pair_flops,
        1,
    )
    (image_sum,) = call(
        next_kernel, [total], (scalars, image_out, image_rows, text_far, image_sum), pair_flops, 1
    )
    half = array((HALF, ROWS), jnp.bfloat16)
    image_dir, keep, send = call(
        image_last_kernel,
        [array((ROWS, D), jnp.bfloat16), half, half],
        (
            scalars, image_out, image_rows, text_near, image_sum, image_unit, image_inv, order
        ),
        pair_flops + 2 * ROWS * D * D,
        1,
    )
    got = swap_cores(send)
    (head,) = call(
        head_kernel,
        [array((8, 96, HALF), jnp.bfloat16)],
        (keep, feat_turned, got, feat_near),
        4 * HALF * ROWS * D,
    )
    head = exchange(head, NEAR_GROUPS)
    head = jnp.sum(head.astype(jnp.float32), axis=0).astype(jnp.bfloat16)
    head = jnp.swapaxes(head.reshape(4, 24, 8, 48), 1, 2).reshape(32, 24, 48)
    head = exchange(head, FAR_GROUPS)
    head_grad = jnp.sum(head.astype(jnp.float32), axis=0).T

    (image_back,) = call(
        back_kernel,
        [array((ROWS, D), jnp.bfloat16)],
        (image_dir, head_weight),
        2 * ROWS * D * D,
    )
    (text_sum,) = call(
        first_kernel,
        [total],
        (scalars, text_out, text_rows, image_out, image_mix),
        2 * pair_flops,
        1,
    )
    (text_sum,) = call(
        next_kernel, [total], (scalars, text_out, text_rows, image_far, text_sum), pair_flops, 1
    )
    (text_back,) = call(
        text_last_kernel,
        [array((ROWS, D), jnp.bfloat16)],
        (scalars, text_out, text_rows, image_near, text_sum, text_emb),
        pair_flops,
        1,
    )
    return (image_back, text_back, head_grad)


def solution(mesh):
    in_specs = (
        P(("blk", "lane"), None),
        P(("blk", "lane"), None),
        P(),
        P(("blk", "lane")),
        P(),
        P(),
        P(),
        P(),
    )
    out_specs = (P(("blk", "lane"), None), P(("blk", "lane"), None), P("lane", "blk"))
    return jax.shard_map(
        on_device, mesh=mesh, in_specs=in_specs, out_specs=out_specs, check_vma=False
    )
```

```python
import jax
import jax.numpy as jnp
from jax import lax
from jax.experimental import pallas as pl
from jax.experimental.pallas import tpu as pltpu
from jax.sharding import PartitionSpec as P

D = 768
HALF = D // 2
ROWS = 384
TAIL = 16
LABELS = 128
N_BLK = 32
EPSILON = 1e-06
VMEM_BYTES = 20 * 1024 * 1024


def device_index(z_hi, x, core, z_lo, y):
    return ((z_hi * 4 + x) * 2 + core) * 16 + z_lo * 8 + y


NEAR_GROUPS = [
    [device_index(z, x, c, l, 2 * y_hi + y_lo) for x in range(4) for y_lo in range(2)]
    for z in range(4)
    for c in range(2)
    for l in range(2)
    for y_hi in range(4)
]
FAR_GROUPS = [
    [
        device_index(z, x, c, l, 2 * y_hi + y_lo)
        for z in range(4)
        for l in range(2)
        for y_hi in range(4)
    ]
    for x in range(4)
    for c in range(2)
    for y_lo in range(2)
]


def permute(value, target):
    pairs = [(i, target(i)) for i in range(N_BLK)]
    return lax.ppermute(value, "blk", [(i, j % N_BLK) for i, j in pairs if j is not None])


def swap_cores(value):
    return permute(value, lambda i: i ^ 1)


def exchange(value, groups):
    return lax.all_to_all(value, ("blk", "lane"), 0, 0, axis_index_groups=groups, tiled=True)


def dot(left, right, dims=((1,), (0,))):
    return lax.dot_general(left, right, (dims, ((), ())), preferred_element_type=jnp.float32)


def call(kernel, micros, outs, args, scalars=0, scratch=(), after=()):
    smem = pl.BlockSpec(memory_space=pltpu.SMEM)
    vmem = pl.BlockSpec(memory_space=pltpu.VMEM)
    anywhere = pl.BlockSpec(memory_space=pl.ANY)
    count, skipped = len(args), len(args) + len(after)

    def body(*refs):
        kernel(*refs[:count], *refs[skipped:])

    return pl.pallas_call(
        body,
        out_shape=outs,
        in_specs=[smem] * scalars + [vmem] * (count - scalars) + [anywhere] * len(after),
        out_specs=[vmem] * len(outs),
        scratch_shapes=scratch,
        cost_estimate=pl.CostEstimate(
            flops=int(micros * 1.1e9), bytes_accessed=int(micros * 3.0e6), transcendentals=0
        ),
        compiler_params=pltpu.CompilerParams(vmem_limit_bytes=VMEM_BYTES),
    )(*args, *after)


def array(shape, dtype):
    return jax.ShapeDtypeStruct(shape, dtype)


def put_langs(langs_ref, out_ref):
    langs = langs_ref[...].astype(jnp.float32)
    row = jnp.concatenate([langs, jnp.zeros((1, D - ROWS), jnp.float32)], axis=1)
    out_ref[ROWS:, :] = jnp.broadcast_to(row, (TAIL, D)).astype(jnp.bfloat16)


def text_kernel(text_ref, langs_ref, out_ref):
    text = text_ref[...].astype(jnp.float32)
    inverse = lax.rsqrt(jnp.sum(text * text, axis=-1, keepdims=True) + EPSILON)
    out_ref[:ROWS, :] = (text * inverse).astype(jnp.bfloat16)
    put_langs(langs_ref, out_ref)


def image_kernel(feat_ref, head_ref, langs_ref, out_ref, unit_ref, inv_ref):
    projected = dot(feat_ref[...], head_ref[...])
    inverse = lax.rsqrt(jnp.sum(projected * projected, axis=-1, keepdims=True) + EPSILON)
    unit = projected * inverse
    unit_ref[...] = unit
    inv_ref[...] = inverse
    out_ref[:ROWS, :] = unit.astype(jnp.bfloat16)
    put_langs(langs_ref, out_ref)


def pair_term(scale, bias, own, own_rows, other_ref, positive):
    other = other_ref[:ROWS, :]
    langs = other_ref[ROWS : ROWS + 1, :ROWS].astype(jnp.int32)
    hot = lax.broadcasted_iota(jnp.int32, (LABELS, ROWS), 0) == langs
    weight = dot(own_rows, hot.astype(jnp.float32).astype(jnp.bfloat16))
    logit = scale * dot(own, other, ((1,), (1,))) + bias
    excess = 0.5 + 0.5 * jnp.tanh(0.5 * logit)
    if positive:
        row = lax.broadcasted_iota(jnp.int32, (ROWS, ROWS), 0)
        column = lax.broadcasted_iota(jnp.int32, (ROWS, ROWS), 1)
        excess = jnp.where(row == column, excess - 1.0, excess)
    return dot((weight * excess).astype(jnp.bfloat16), other)


def own_kernel(
    scalar_ref, image_ref, image_rows_ref, text_ref, text_rows_ref, image_sum_ref, text_sum_ref
):
    scale, bias = scalar_ref[0], scalar_ref[1]
    image_sum_ref[...] = pair_term(
        scale, bias, image_ref[:ROWS, :], image_rows_ref[...], text_ref, True
    )
    text_sum_ref[...] = pair_term(
        scale, bias, text_ref[:ROWS, :], text_rows_ref[...], image_ref, True
    )


def middle_kernel(
    scalar_ref, own_ref, rows_ref, mix_ref, far_ref, near_ref, before_ref, sum_ref
):
    scale, bias = scalar_ref[0], scalar_ref[1]
    own, rows = own_ref[:ROWS, :], rows_ref[...]
    sum_ref[...] = before_ref[...]

    @pl.when(scalar_ref[4] == 0.0)
    def _():
        sum_ref[...] += pair_term(scale, bias, own, rows, mix_ref, False)

    @pl.when(scalar_ref[3] == 0.0)
    def _():
        sum_ref[...] += pair_term(scale, bias, own, rows, far_ref, False)

    @pl.when(scalar_ref[2] == 0.0)
    def _():
        sum_ref[...] += pair_term(scale, bias, own, rows, near_ref, False)


def last_sum(
    scalar_ref, own_ref, rows_ref, hop_ref, skip_ref, corner_ref, before_ref, block_ref, sum_ref
):
    scale, bias = scalar_ref[0], scalar_ref[1]
    sum_ref[...] = before_ref[...]

    @pl.when(scalar_ref[2] > 0.0)
    def _():
        block_ref[...] = corner_ref[...]

    @pl.when(scalar_ref[3] > 0.0)
    def _():
        block_ref[...] = hop_ref[...]

    @pl.when(scalar_ref[4] > 0.0)
    def _():
        block_ref[...] = skip_ref[...]

    @pl.when(scalar_ref[2] + scalar_ref[3] + scalar_ref[4] > 0.0)
    def _():
        own, rows = own_ref[:ROWS, :], rows_ref[...]
        sum_ref[...] += pair_term(scale, bias, own, rows, block_ref, False)

    return scale * sum_ref[...]


def image_last_kernel(
    scalar_ref, own_ref, rows_ref, hop_ref, skip_ref, corner_ref, before_ref, unit_ref, inv_ref,
    order_ref, dir_ref, keep_ref, send_ref, block_ref, sum_ref,
):
    grad = last_sum(
        scalar_ref, own_ref, rows_ref, hop_ref, skip_ref, corner_ref, before_ref, block_ref,
        sum_ref,
    )
    unit = unit_ref[...]
    radial = jnp.sum(unit * grad, axis=-1, keepdims=True)
    direction = ((grad - unit * radial) * inv_ref[...]).astype(jnp.bfloat16)
    dir_ref[...] = direction
    turned = dot(order_ref[...], direction, ((1,), (1,))).astype(jnp.bfloat16)
    keep_ref[...] = turned[:HALF, :]
    send_ref[...] = turned[HALF:, :]


def text_last_kernel(
    scalar_ref, own_ref, rows_ref, hop_ref, skip_ref, corner_ref, before_ref, text_ref, out_ref,
    block_ref, sum_ref,
):
    grad = last_sum(
        scalar_ref, own_ref, rows_ref, hop_ref, skip_ref, corner_ref, before_ref, block_ref,
        sum_ref,
    )
    text = text_ref[...].astype(jnp.float32)
    inverse = lax.rsqrt(jnp.sum(text * text, axis=-1, keepdims=True) + EPSILON)
    unit = text * inverse
    radial = jnp.sum(unit * grad, axis=-1, keepdims=True)
    out_ref[...] = ((grad - unit * radial) * inverse).astype(jnp.bfloat16)


def head_kernel(keep_ref, got_ref, feat_ref, out_ref, both_ref):
    both_ref[:, :ROWS] = keep_ref[...]
    both_ref[:, ROWS:] = got_ref[...]
    for y_lo in range(2):
        head = dot(both_ref[...], feat_ref[:, HALF * y_lo : HALF * y_lo + HALF])
        for x in range(4):
            out_ref[2 * x + y_lo] = head[96 * x : 96 * x + 96, :].astype(jnp.bfloat16)


def back_kernel(dir_ref, head_ref, out_ref):
    out_ref[...] = dot(dir_ref[...], head_ref[...], ((1,), (1,))).astype(jnp.bfloat16)


def column_order(core):
    new = jnp.arange(D, dtype=jnp.int32)
    side, x, z_hi, rest = new // 384, new // 96 % 4, new // 24 % 4, new % 24
    return z_hi * 192 + x * 48 + (side ^ core) * 24 + rest


def row_order():
    new = jnp.arange(D, dtype=jnp.int32)
    y_lo, z_lo, y_hi, rest = new // 384, new // 192 % 2, new // 48 % 4, new % 48
    return z_lo * 384 + (y_hi * 2 + y_lo) * 48 + rest


def order_matrix(old):
    return (old[:, None] == jnp.arange(D, dtype=jnp.int32)[None, :]).astype(jnp.bfloat16)


def on_device(
    image_feat, text_emb, head_weight, lang_ids, pair_mask, weight_codes, log_scale, logit_bias
):
    place = lax.axis_index("blk") % 8
    lang_count = pair_mask.shape[0]
    allowed = jnp.maximum(pair_mask, jnp.eye(lang_count, dtype=jnp.int32)).astype(jnp.float32)
    codes = weight_codes.astype(jnp.float32)
    table = (allowed * (0.25 * (codes[:, None] + codes[None, :]))).astype(jnp.bfloat16)
    extra = LABELS - lang_count
    table = jnp.pad(table, ((0, extra), (0, extra)))
    scale = jnp.exp(log_scale)
    text_scalars, image_scalars = [
        jnp.stack([scale, logit_bias] + [flag.astype(jnp.float32) for flag in flags])
        for flags in (
            [place == 0, place == 1, place == 2],
            [place == 7, place == 6, place == 5],
        )
    ]
    langs = lang_ids.reshape(1, ROWS)
    block = array((ROWS + TAIL, D), jnp.bfloat16)
    total = array((ROWS, D), jnp.float32)
    scratch = [pltpu.VMEM(block.shape, block.dtype), pltpu.VMEM(total.shape, total.dtype)]

    (text_out,) = call(text_kernel, 0.3, [block], (text_emb, langs))
    text_far = permute(text_out, lambda i: i + 2 if i % 8 != 7 else i - 6)
    text_mix = permute(
        text_out, lambda i: i + 1 if i % 2 == 0 else (i + 3 if i % 8 != 7 else i - 5)
    )

    image_out, image_unit, image_inv = call(
        image_kernel,
        1.0,
        [block, total, array((ROWS, 1), jnp.float32)],
        (image_feat, head_weight, langs),
    )
    image_far = permute(image_out, lambda i: i - 2 if i % 8 != 0 else i + 6)
    image_mix = permute(
        image_out, lambda i: i - 1 if i % 2 == 1 else (i - 3 if i % 8 != 0 else i + 5)
    )

    own_hot = (lang_ids[:, None] == jnp.arange(LABELS)[None, :]).astype(jnp.bfloat16)
    image_rows = dot(own_hot, table).astype(jnp.bfloat16)
    text_rows = dot(own_hot, table, ((1,), (1,))).astype(jnp.bfloat16)
    feat_turned = dot(image_feat, order_matrix(row_order()), ((1,), (1,))).astype(jnp.bfloat16)
    feat_near = swap_cores(feat_turned)
    feat_both = jnp.concatenate([feat_turned, feat_near], axis=0)
    order = order_matrix(column_order(place % 2))
    image_sum, text_sum = call(
        own_kernel,
        2.6,
        [total, total],
        (text_scalars, image_out, image_rows, text_out, text_rows),
        1,
    )
    text_far, text_mix, image_sum, text_sum, feat_both, order = lax.optimization_barrier(
        (text_far, text_mix, image_sum, text_sum, feat_both, order)
    )

    text_hop = permute(text_far, lambda i: {1: i + 8}.get(i % 8))
    text_near = permute(text_far, lambda i: i ^ 1 if i % 8 != 1 else None)
    text_skip = permute(text_mix, lambda i: {2: i + 8}.get(i % 8))
    image_hop = permute(image_far, lambda i: {6: i - 8}.get(i % 8))
    image_near = permute(image_far, lambda i: i ^ 1 if i % 8 != 6 else None)
    image_skip = permute(image_mix, lambda i: {5: i - 8}.get(i % 8))
    (image_sum,) = call(
        middle_kernel,
        4.0,
        [total],
        (text_scalars, image_out, image_rows, text_mix, text_far, text_near, image_sum),
        1,
        (),
        (image_far, image_mix),
    )
    text_hop, text_skip, image_sum = lax.optimization_barrier((text_hop, text_skip, image_sum))
    text_corner = permute(text_hop, lambda i: {1: i - 1}.get(i % 8))
    half = array((HALF, ROWS), jnp.bfloat16)
    image_dir, keep, send = call(
        image_last_kernel,
        3.0,
        [array((ROWS, D), jnp.bfloat16), half, half],
        (
            text_scalars, image_out, image_rows, text_hop, text_skip, text_corner, image_sum,
            image_unit, image_inv, order,
        ),
        1,
        scratch,
        (image_hop, image_near, image_skip),
    )
    got = swap_cores(send)
    (head,) = call(
        head_kernel,
        1.5,
        [array((8, 96, HALF), jnp.bfloat16)],
        (keep, got, feat_both),
        0,
        [pltpu.VMEM((HALF, D), jnp.bfloat16)],
    )
    head = exchange(head, NEAR_GROUPS)
    image_corner = permute(image_hop, lambda i: {6: i + 1}.get(i % 8))
    head = jnp.sum(head.astype(jnp.float32), axis=0).astype(jnp.bfloat16)
    head = jnp.swapaxes(head.reshape(4, 24, 8, 48), 1, 2).reshape(32, 24, 48)
    head = exchange(head, FAR_GROUPS)
    head_grad = jnp.sum(head.astype(jnp.float32), axis=0).T

    (image_back,) = call(
        back_kernel, 1.5, [array((ROWS, D), jnp.bfloat16)], (image_dir, head_weight)
    )
    (text_sum,) = call(
        middle_kernel,
        4.0,
        [total],
        (image_scalars, text_out, text_rows, image_mix, image_far, image_near, text_sum),
        1,
    )
    (text_back,) = call(
        text_last_kernel,
        3.0,
        [array((ROWS, D), jnp.bfloat16)],
        (
            image_scalars, text_out, text_rows, image_hop, image_skip, image_corner, text_sum,
            text_emb,
        ),
        1,
        scratch,
    )
    return (image_back, text_back, head_grad)


def solution(mesh):
    in_specs = (
        P(("blk", "lane"), None),
        P(("blk", "lane"), None),
        P(),
        P(("blk", "lane")),
        P(),
        P(),
        P(),
        P(),
    )
    out_specs = (P(("blk", "lane"), None), P(("blk", "lane"), None), P("lane", "blk"))
    return jax.shard_map(
        on_device, mesh=mesh, in_specs=in_specs, out_specs=out_specs, check_vma=False
    )
```

```python
import jax
import jax.numpy as jnp
from jax import lax
from jax.experimental import pallas as pl
from jax.experimental.pallas import tpu as pltpu
from jax.sharding import PartitionSpec as P

D = 768
HALF = D // 2
ROWS = 384
TAIL = 16
LABELS = 128
N_BLK = 32
EPSILON = 1e-06
VMEM_BYTES = 20 * 1024 * 1024


def device_index(z_hi, x, core, z_lo, y):
    return ((z_hi * 4 + x) * 2 + core) * 16 + z_lo * 8 + y


NEAR_GROUPS = [
    [device_index(z_hi, x, core, z_lo, 2 * y_hi + y_lo) for x in range(4) for y_lo in range(2)]
    for z_hi in range(4)
    for core in range(2)
    for z_lo in range(2)
    for y_hi in range(4)
]
FAR_GROUPS = [
    [
        device_index(z_hi, x, core, z_lo, 2 * y_hi + y_lo)
        for z_hi in range(4)
        for z_lo in range(2)
        for y_hi in range(4)
    ]
    for x in range(4)
    for core in range(2)
    for y_lo in range(2)
]


def permute(value, target):
    pairs = [(i, target(i)) for i in range(N_BLK)]
    return lax.ppermute(value, "blk", [(i, j % N_BLK) for i, j in pairs if j is not None])


def swap_cores(value):
    return permute(value, lambda i: i ^ 1)


def exchange(value, groups):
    return lax.all_to_all(value, ("blk", "lane"), 0, 0, axis_index_groups=groups, tiled=True)


def dot(left, right, dims=((1,), (0,))):
    return lax.dot_general(left, right, (dims, ((), ())), preferred_element_type=jnp.float32)


def call(kernel, micros, outs, args, scalars=0, scratch=(), after=()):
    smem = pl.BlockSpec(memory_space=pltpu.SMEM)
    vmem = pl.BlockSpec(memory_space=pltpu.VMEM)
    args = list(args)
    if after:
        args[scalars] = lax.optimization_barrier((args[scalars], *after))[0]
    return pl.pallas_call(
        kernel,
        out_shape=outs,
        in_specs=[smem] * scalars + [vmem] * (len(args) - scalars),
        out_specs=[vmem] * len(outs),
        scratch_shapes=scratch,
        cost_estimate=pl.CostEstimate(
            flops=int(micros * 1.1e9), bytes_accessed=int(micros * 3.0e6), transcendentals=0
        ),
        compiler_params=pltpu.CompilerParams(vmem_limit_bytes=VMEM_BYTES),
    )(*args)


def pick(index, first, second, third):
    anywhere = pl.BlockSpec(memory_space=pl.ANY)
    return pl.pallas_call(
        pick_kernel,
        out_shape=array(first.shape, first.dtype),
        in_specs=[pl.BlockSpec(memory_space=pltpu.SMEM)] + [anywhere] * 3,
        out_specs=pl.BlockSpec(memory_space=pltpu.VMEM),
        scratch_shapes=[pltpu.SemaphoreType.DMA(())],
        cost_estimate=pl.CostEstimate(flops=0, bytes_accessed=3000000, transcendentals=0),
    )(index, first, second, third)


def array(shape, dtype):
    return jax.ShapeDtypeStruct(shape, dtype)


def put_langs(langs_ref, out_ref):
    langs = langs_ref[...].astype(jnp.float32)
    row = jnp.concatenate([langs, jnp.zeros((1, D - ROWS), jnp.float32)], axis=1)
    out_ref[ROWS:, :] = jnp.broadcast_to(row, (TAIL, D)).astype(jnp.bfloat16)


def text_kernel(text_ref, langs_ref, out_ref):
    text = text_ref[...].astype(jnp.float32)
    inverse = lax.rsqrt(jnp.sum(text * text, axis=-1, keepdims=True) + EPSILON)
    out_ref[:ROWS, :] = (text * inverse).astype(jnp.bfloat16)
    put_langs(langs_ref, out_ref)


def image_kernel(feat_ref, head_ref, langs_ref, out_ref, inv_ref):
    projected = dot(feat_ref[...], head_ref[...])
    inverse = lax.rsqrt(jnp.sum(projected * projected, axis=-1, keepdims=True) + EPSILON)
    inv_ref[...] = inverse
    out_ref[:ROWS, :] = (projected * inverse).astype(jnp.bfloat16)
    put_langs(langs_ref, out_ref)


def pair_term(scale, bias, own, own_rows, other_ref, positive):
    other = other_ref[:ROWS, :]
    langs = other_ref[ROWS : ROWS + 1, :ROWS].astype(jnp.int32)
    hot = lax.broadcasted_iota(jnp.int32, (LABELS, ROWS), 0) == langs
    weight = dot(own_rows, hot.astype(jnp.float32).astype(jnp.bfloat16))
    logit = scale * dot(own, other, ((1,), (1,))) + bias
    excess = 0.5 + 0.5 * jnp.tanh(0.5 * logit)
    if positive:
        row = lax.broadcasted_iota(jnp.int32, (ROWS, ROWS), 0)
        column = lax.broadcasted_iota(jnp.int32, (ROWS, ROWS), 1)
        excess = jnp.where(row == column, excess - 1.0, excess)
    return dot((weight * excess).astype(jnp.bfloat16), other)


def own_kernel(scalar_ref, own_ref, rows_ref, other_ref, sum_ref):
    sum_ref[...] = pair_term(
        scalar_ref[0], scalar_ref[1], own_ref[:ROWS, :], rows_ref[...], other_ref, True
    )


def add_term(scalar_ref, own_ref, rows_ref, other_ref, off, sum_ref):
    @pl.when(off == 0.0)
    def _():
        sum_ref[...] += pair_term(
            scalar_ref[0], scalar_ref[1], own_ref[:ROWS, :], rows_ref[...], other_ref, False
        )


def middle_kernel(scalar_ref, own_ref, rows_ref, mix_ref, far_ref, before_ref, sum_ref):
    sum_ref[...] = before_ref[...]
    add_term(scalar_ref, own_ref, rows_ref, mix_ref, scalar_ref[2], sum_ref)
    add_term(scalar_ref, own_ref, rows_ref, far_ref, scalar_ref[3], sum_ref)


def pick_kernel(pick_ref, first_ref, second_ref, third_ref, out_ref, sem_ref):
    for index, ref in enumerate((first_ref, second_ref, third_ref)):

        @pl.when(pick_ref[0] == index)
        def _():
            copy = pltpu.make_async_copy(ref, out_ref, sem_ref)
            copy.start()
            copy.wait()


def image_last_kernel(
    scalar_ref, own_ref, rows_ref, near_ref, hop_ref, skip_ref, direct_ref, before_ref, inv_ref,
    order_ref, dir_ref, keep_ref, send_ref, sum_ref,
):
    sum_ref[...] = before_ref[...]
    add_term(scalar_ref, own_ref, rows_ref, near_ref, scalar_ref[4], sum_ref)
    add_term(scalar_ref, own_ref, rows_ref, hop_ref, scalar_ref[6], sum_ref)
    add_term(scalar_ref, own_ref, rows_ref, skip_ref, scalar_ref[7], sum_ref)
    add_term(scalar_ref, own_ref, rows_ref, direct_ref, 1.0 - scalar_ref[4], sum_ref)
    grad = scalar_ref[0] * sum_ref[...]
    unit = own_ref[:ROWS, :].astype(jnp.float32)
    radial = jnp.sum(unit * grad, axis=-1, keepdims=True)
    direction = ((grad - unit * radial) * inv_ref[...]).astype(jnp.bfloat16)
    dir_ref[...] = direction
    turned = dot(order_ref[...], direction, ((1,), (1,))).astype(jnp.bfloat16)
    keep_ref[...] = turned[:HALF, :]
    send_ref[...] = turned[HALF:, :]


def text_back_kernel(
    scalar_ref, own_ref, rows_ref, same_ref, mix_ref, far_ref, near_ref, late_ref, text_ref,
    out_ref, sum_ref,
):
    own_kernel(scalar_ref, own_ref, rows_ref, same_ref, sum_ref)
    add_term(scalar_ref, own_ref, rows_ref, mix_ref, scalar_ref[2], sum_ref)
    add_term(scalar_ref, own_ref, rows_ref, far_ref, scalar_ref[3], sum_ref)
    add_term(scalar_ref, own_ref, rows_ref, near_ref, scalar_ref[4], sum_ref)
    add_term(scalar_ref, own_ref, rows_ref, late_ref, scalar_ref[5], sum_ref)
    grad = scalar_ref[0] * sum_ref[...]
    text = text_ref[...].astype(jnp.float32)
    inverse = lax.rsqrt(jnp.sum(text * text, axis=-1, keepdims=True) + EPSILON)
    unit = text * inverse
    radial = jnp.sum(unit * grad, axis=-1, keepdims=True)
    out_ref[...] = ((grad - unit * radial) * inverse).astype(jnp.bfloat16)


def head_kernel(keep_ref, got_ref, feat_ref, feat_near_ref, out_ref):
    for y_lo in range(2):
        columns = slice(HALF * y_lo, HALF * y_lo + HALF)
        head = dot(keep_ref[...], feat_ref[:, columns])
        head += dot(got_ref[...], feat_near_ref[:, columns])
        for x in range(4):
            out_ref[2 * x + y_lo] = head[96 * x : 96 * x + 96, :].astype(jnp.bfloat16)


def near_sum_kernel(parts_ref, out_ref):
    total = parts_ref[0].astype(jnp.float32)
    for k in range(1, 8):
        total += parts_ref[k].astype(jnp.float32)
    for z_hi in range(4):
        for k in range(8):
            piece = total[24 * z_hi : 24 * z_hi + 24, 48 * k : 48 * k + 48]
            blank = jnp.zeros((8, 32), jnp.float32)
            upper = jnp.concatenate([piece[:8], piece[8:16], blank], axis=1)
            lower = jnp.concatenate([piece[16:], piece[16:], blank], axis=1)
            packed = jnp.concatenate([upper, lower], axis=0)
            out_ref[8 * z_hi + k] = packed.astype(jnp.bfloat16)


def far_sum_kernel(parts_ref, out_ref):
    total = parts_ref[0].astype(jnp.float32)
    for k in range(1, 32):
        total += parts_ref[k].astype(jnp.float32)
    head = jnp.concatenate([total[:8, :48], total[:8, 48:96], total[8:, :48]], axis=0)
    out_ref[...] = head


def back_kernel(dir_ref, head_ref, out_ref):
    out_ref[...] = dot(dir_ref[...], head_ref[...], ((1,), (1,))).astype(jnp.bfloat16)


def column_order(core):
    new = jnp.arange(D, dtype=jnp.int32)
    side, x, z_hi, rest = new // 384, new // 96 % 4, new // 24 % 4, new % 24
    return z_hi * 192 + x * 48 + (side ^ core) * 24 + rest


def row_order():
    new = jnp.arange(D, dtype=jnp.int32)
    y_lo, z_lo, y_hi, rest = new // 384, new // 192 % 2, new // 48 % 4, new % 48
    return z_lo * 384 + (y_hi * 2 + y_lo) * 48 + rest


def order_matrix(old):
    return (old[:, None] == jnp.arange(D, dtype=jnp.int32)[None, :]).astype(jnp.bfloat16)


def on_device(
    image_feat, text_emb, head_weight, lang_ids, pair_mask, weight_codes, log_scale, logit_bias
):
    place = lax.axis_index("blk") % 8
    lang_count = pair_mask.shape[0]
    allowed = jnp.maximum(pair_mask, jnp.eye(lang_count, dtype=jnp.int32)).astype(jnp.float32)
    codes = weight_codes.astype(jnp.float32)
    table = (allowed * (0.25 * (codes[:, None] + codes[None, :]))).astype(jnp.bfloat16)
    extra = LABELS - lang_count
    table = jnp.pad(table, ((0, extra), (0, extra)))
    scale = jnp.exp(log_scale)
    text_scalars, image_scalars = [
        jnp.stack([scale, logit_bias] + [flag.astype(jnp.float32) for flag in flags])
        for flags in (
            [
                relay | inner, spot == 1, spot == 0, (spot % 2 == 1) & (spot != 1),
                (spot != 1) & ~inner, ~relay,
            ]
            for spot, relay, inner in [
                (spot, spot == 2, (spot == 4) | (spot == 6)) for spot in (place, 7 - place)
            ]
        )
    ]
    image_pick = jnp.where(place == 0, 2, jnp.where(place == 5, 1, 0)).reshape(1)
    langs = lang_ids.reshape(1, ROWS)
    block = array((ROWS + TAIL, D), jnp.bfloat16)
    total = array((ROWS, D), jnp.float32)
    scratch = [pltpu.VMEM(total.shape, total.dtype)]

    (text_out,) = call(text_kernel, 0.3, [block], (text_emb, langs))
    text_far = permute(text_out, lambda i: i + 2 if i % 8 != 7 else i - 6)
    text_mix = permute(
        text_out, lambda i: i + 1 if i % 2 == 0 else {5: i + 3, 7: i - 5}.get(i % 8)
    )

    image_out, image_inv = call(
        image_kernel,
        1.0,
        [block, array((ROWS, 1), jnp.float32)],
        (image_feat, head_weight, langs),
    )
    image_far = permute(image_out, lambda i: i - 2 if i % 8 != 0 else i + 6)
    image_mix = permute(
        image_out, lambda i: i - 1 if i % 2 == 1 else {2: i - 3, 0: i + 5}.get(i % 8)
    )

    own_hot = (lang_ids[:, None] == jnp.arange(LABELS)[None, :]).astype(jnp.bfloat16)
    image_rows = dot(own_hot, table).astype(jnp.bfloat16)
    text_rows = dot(own_hot, table, ((1,), (1,))).astype(jnp.bfloat16)
    feat_turned = dot(image_feat, order_matrix(row_order()), ((1,), (1,))).astype(jnp.bfloat16)
    feat_near = swap_cores(feat_turned)
    order = order_matrix(column_order(place % 2))
    (image_sum,) = call(
        own_kernel, 1.5, [total], (text_scalars, image_out, image_rows, text_out), 1
    )
    text_far, text_own, feat_near, image_sum, order = lax.optimization_barrier(
        (text_far, text_out, feat_near, image_sum, order)
    )

    text_near = permute(text_far, lambda i: i ^ 1 if i % 8 != 1 else None)
    text_hop = permute(text_far, lambda i: {1: i + 8, 3: i + 1, 5: i + 1}.get(i % 8))
    text_skip = permute(text_mix, lambda i: {2: i + 8}.get(i % 8))
    text_direct = permute(text_own, lambda i: {7: i + 1}.get(i % 8))
    (image_sum,) = call(
        middle_kernel,
        2.6,
        [total],
        (text_scalars, image_out, image_rows, text_mix, text_far, image_sum),
        1,
    )
    image_pass = pick(image_pick, image_far, image_mix, image_out)
    image_late = permute(
        image_pass, lambda i: {6: i - 8, 5: i - 8, 4: i - 1, 2: i - 1, 0: i - 1}.get(i % 8)
    )
    image_near = permute(image_far, lambda i: i ^ 1 if i % 8 != 6 else None)
    half = array((HALF, ROWS), jnp.bfloat16)
    image_dir, keep, send = call(
        image_last_kernel,
        0.01,
        [array((ROWS, D), jnp.bfloat16), half, half],
        (
            text_scalars, image_out, image_rows, text_near, text_hop, text_skip, text_direct,
            image_sum, image_inv, order,
        ),
        1,
        scratch,
    )
    got = swap_cores(send)
    (head,) = call(
        head_kernel,
        0.01,
        [array((8, 96, HALF), jnp.bfloat16)],
        (keep, got, feat_turned, feat_near),
        after=(image_late, image_near),
    )
    sent = head
    head = exchange(head, NEAR_GROUPS)
    (text_back,) = call(
        text_back_kernel,
        6.0,
        [array((ROWS, D), jnp.bfloat16)],
        (
            image_scalars, text_out, text_rows, image_out, image_mix, image_far, image_near,
            image_late, text_emb,
        ),
        1,
        scratch,
        (sent,),
    )
    (head,) = call(
        near_sum_kernel,
        0.5,
        [array((32, 16, 128), jnp.bfloat16)],
        (head,),
        after=(text_back,),
    )
    near_done = head
    head = exchange(head, FAR_GROUPS)
    (head_grad,) = call(far_sum_kernel, 0.5, [array((24, 48), jnp.float32)], (head,))

    (image_back,) = call(
        back_kernel,
        1.5,
        [array((ROWS, D), jnp.bfloat16)],
        (image_dir, head_weight),
        after=(near_done,),
    )
    return (image_back, text_back, head_grad.T)


def solution(mesh):
    in_specs = (
        P(("blk", "lane"), None),
        P(("blk", "lane"), None),
        P(),
        P(("blk", "lane")),
        P(),
        P(),
        P(),
        P(),
    )
    out_specs = (P(("blk", "lane"), None), P(("blk", "lane"), None), P("lane", "blk"))
    return jax.shard_map(
        on_device, mesh=mesh, in_specs=in_specs, out_specs=out_specs, check_vma=False
    )
```

```python
import jax
import jax.numpy as jnp
from jax import lax
from jax.experimental import pallas as pl
from jax.experimental.pallas import tpu as pltpu
from jax.sharding import PartitionSpec as P

D = 768
HALF = D // 2
ROWS = 384
TAIL = 16
LABELS = 128
N_BLK = 32
EPSILON = 1e-06
VMEM_BYTES = 20 * 1024 * 1024


def device_index(z_hi, x, core, z_lo, y):
    return ((z_hi * 4 + x) * 2 + core) * 16 + z_lo * 8 + y


NEAR_GROUPS = [
    [device_index(z_hi, x, core, z_lo, 2 * y_hi + y_lo) for x in range(4) for y_lo in range(2)]
    for z_hi in range(4)
    for core in range(2)
    for z_lo in range(2)
    for y_hi in range(4)
]
FAR_GROUPS = [
    [
        device_index(z_hi, x, core, z_lo, 2 * y_hi + y_lo)
        for z_hi in range(4)
        for z_lo in range(2)
        for y_hi in range(4)
    ]
    for x in range(4)
    for core in range(2)
    for y_lo in range(2)
]


def permute(value, target):
    pairs = [(i, target(i)) for i in range(N_BLK)]
    return lax.ppermute(value, "blk", [(i, j % N_BLK) for i, j in pairs if j is not None])


def swap_cores(value):
    return permute(value, lambda i: i ^ 1)


def exchange(value, groups):
    return lax.all_to_all(value, ("blk", "lane"), 0, 0, axis_index_groups=groups, tiled=True)


def dot(left, right, dims=((1,), (0,))):
    return lax.dot_general(left, right, (dims, ((), ())), preferred_element_type=jnp.float32)


def call(kernel, micros, outs, args, scalars=0, scratch=()):
    smem = pl.BlockSpec(memory_space=pltpu.SMEM)
    vmem = pl.BlockSpec(memory_space=pltpu.VMEM)
    return pl.pallas_call(
        kernel,
        out_shape=outs,
        in_specs=[smem] * scalars + [vmem] * (len(args) - scalars),
        out_specs=[vmem] * len(outs),
        scratch_shapes=scratch,
        cost_estimate=pl.CostEstimate(
            flops=int(micros * 1.1e9), bytes_accessed=int(micros * 3.0e6), transcendentals=0
        ),
        compiler_params=pltpu.CompilerParams(vmem_limit_bytes=VMEM_BYTES),
    )(*args)


def pick(index, first, second, third):
    anywhere = pl.BlockSpec(memory_space=pl.ANY)
    return pl.pallas_call(
        pick_kernel,
        out_shape=array(first.shape, first.dtype),
        in_specs=[pl.BlockSpec(memory_space=pltpu.SMEM)] + [anywhere] * 3,
        out_specs=pl.BlockSpec(memory_space=pltpu.VMEM),
        scratch_shapes=[pltpu.SemaphoreType.DMA(())],
        cost_estimate=pl.CostEstimate(flops=0, bytes_accessed=3000000, transcendentals=0),
    )(index, first, second, third)


def array(shape, dtype):
    return jax.ShapeDtypeStruct(shape, dtype)


def put_langs(langs_ref, out_ref):
    langs = langs_ref[...].astype(jnp.float32)
    row = jnp.concatenate([langs, jnp.zeros((1, D - ROWS), jnp.float32)], axis=1)
    out_ref[ROWS:, :] = jnp.broadcast_to(row, (TAIL, D)).astype(jnp.bfloat16)


def text_kernel(text_ref, langs_ref, out_ref):
    text = text_ref[...].astype(jnp.float32)
    inverse = lax.rsqrt(jnp.sum(text * text, axis=-1, keepdims=True) + EPSILON)
    out_ref[:ROWS, :] = (text * inverse).astype(jnp.bfloat16)
    put_langs(langs_ref, out_ref)


def image_kernel(feat_ref, head_ref, langs_ref, out_ref, inv_ref):
    projected = dot(feat_ref[...], head_ref[...])
    inverse = lax.rsqrt(jnp.sum(projected * projected, axis=-1, keepdims=True) + EPSILON)
    inv_ref[...] = inverse
    out_ref[:ROWS, :] = (projected * inverse).astype(jnp.bfloat16)
    put_langs(langs_ref, out_ref)


def pair_term(scale, bias, own, own_rows, other_ref, positive):
    other = other_ref[:ROWS, :]
    langs = other_ref[ROWS : ROWS + 1, :ROWS].astype(jnp.int32)
    hot = lax.broadcasted_iota(jnp.int32, (LABELS, ROWS), 0) == langs
    weight = dot(own_rows, hot.astype(jnp.float32).astype(jnp.bfloat16))
    logit = scale * dot(own, other, ((1,), (1,))) + bias
    excess = 0.5 + 0.5 * jnp.tanh(0.5 * logit)
    if positive:
        row = lax.broadcasted_iota(jnp.int32, (ROWS, ROWS), 0)
        column = lax.broadcasted_iota(jnp.int32, (ROWS, ROWS), 1)
        excess = jnp.where(row == column, excess - 1.0, excess)
    return dot((weight * excess).astype(jnp.bfloat16), other)


def own_kernel(scalar_ref, own_ref, rows_ref, other_ref, sum_ref):
    sum_ref[...] = pair_term(
        scalar_ref[0], scalar_ref[1], own_ref[:ROWS, :], rows_ref[...], other_ref, True
    )


def add_term(scalar_ref, own_ref, rows_ref, other_ref, off, sum_ref):
    @pl.when(off == 0.0)
    def _():
        sum_ref[...] += pair_term(
            scalar_ref[0], scalar_ref[1], own_ref[:ROWS, :], rows_ref[...], other_ref, False
        )


def middle_kernel(scalar_ref, own_ref, rows_ref, mix_ref, far_ref, before_ref, sum_ref):
    sum_ref[...] = before_ref[...]
    add_term(scalar_ref, own_ref, rows_ref, mix_ref, scalar_ref[2], sum_ref)
    add_term(scalar_ref, own_ref, rows_ref, far_ref, scalar_ref[3], sum_ref)


def near_kernel(scalar_ref, own_ref, rows_ref, near_ref, before_ref, sum_ref):
    sum_ref[...] = before_ref[...]
    add_term(scalar_ref, own_ref, rows_ref, near_ref, scalar_ref[4], sum_ref)


def pick_kernel(pick_ref, first_ref, second_ref, third_ref, out_ref, sem_ref):
    for index, ref in enumerate((first_ref, second_ref, third_ref)):

        @pl.when(pick_ref[0] == index)
        def _():
            copy = pltpu.make_async_copy(ref, out_ref, sem_ref)
            copy.start()
            copy.wait()


def image_last_kernel(
    scalar_ref, own_ref, rows_ref, hop_ref, skip_ref, corner_ref, before_ref, inv_ref, order_ref,
    dir_ref, keep_ref, send_ref, sum_ref,
):
    sum_ref[...] = before_ref[...]
    add_term(scalar_ref, own_ref, rows_ref, hop_ref, scalar_ref[6], sum_ref)
    add_term(scalar_ref, own_ref, rows_ref, skip_ref, scalar_ref[7], sum_ref)
    add_term(scalar_ref, own_ref, rows_ref, corner_ref, 1.0 - scalar_ref[4], sum_ref)
    grad = scalar_ref[0] * sum_ref[...]
    unit = own_ref[:ROWS, :].astype(jnp.float32)
    radial = jnp.sum(unit * grad, axis=-1, keepdims=True)
    direction = ((grad - unit * radial) * inv_ref[...]).astype(jnp.bfloat16)
    dir_ref[...] = direction
    turned = dot(order_ref[...], direction, ((1,), (1,))).astype(jnp.bfloat16)
    keep_ref[...] = turned[:HALF, :]
    send_ref[...] = turned[HALF:, :]


def text_middle_kernel(
    scalar_ref, own_ref, rows_ref, same_ref, mix_ref, far_ref, near_ref, sum_ref
):
    own_kernel(scalar_ref, own_ref, rows_ref, same_ref, sum_ref)
    add_term(scalar_ref, own_ref, rows_ref, mix_ref, scalar_ref[2], sum_ref)
    add_term(scalar_ref, own_ref, rows_ref, far_ref, scalar_ref[3], sum_ref)
    add_term(scalar_ref, own_ref, rows_ref, near_ref, scalar_ref[4], sum_ref)


def text_last_kernel(
    scalar_ref, own_ref, rows_ref, late_ref, before_ref, text_ref, out_ref, sum_ref
):
    sum_ref[...] = before_ref[...]
    add_term(scalar_ref, own_ref, rows_ref, late_ref, scalar_ref[5], sum_ref)
    grad = scalar_ref[0] * sum_ref[...]
    text = text_ref[...].astype(jnp.float32)
    inverse = lax.rsqrt(jnp.sum(text * text, axis=-1, keepdims=True) + EPSILON)
    unit = text * inverse
    radial = jnp.sum(unit * grad, axis=-1, keepdims=True)
    out_ref[...] = ((grad - unit * radial) * inverse).astype(jnp.bfloat16)


def head_kernel(keep_ref, got_ref, feat_ref, feat_near_ref, out_ref):
    head = dot(keep_ref[...], feat_ref[...]) + dot(got_ref[...], feat_near_ref[...])
    for x in range(4):
        out_ref[x, 0] = head[96 * x : 96 * x + 96, :].astype(jnp.bfloat16)


def head_product(keep, got, feat, feat_near):
    whole = pl.BlockSpec((HALF, ROWS), lambda y_lo: (0, 0))
    side = pl.BlockSpec((ROWS, HALF), lambda y_lo: (0, y_lo))
    head = pl.pallas_call(
        head_kernel,
        grid=(2,),
        out_shape=array((4, 2, 96, HALF), jnp.bfloat16),
        in_specs=[whole, whole, side, side],
        out_specs=pl.BlockSpec((4, 1, 96, HALF), lambda y_lo: (0, y_lo, 0, 0)),
        cost_estimate=pl.CostEstimate(
            flops=int(1.9e9), bytes_accessed=int(5.1e6), transcendentals=0
        ),
        compiler_params=pltpu.CompilerParams(vmem_limit_bytes=VMEM_BYTES),
    )(keep, got, feat, feat_near)
    return head.reshape(8, 96, HALF)


def near_sum_kernel(parts_ref, out_ref):
    total = parts_ref[0].astype(jnp.float32)
    for k in range(1, 8):
        total += parts_ref[k].astype(jnp.float32)
    for z_hi in range(4):
        for k in range(8):
            piece = total[24 * z_hi : 24 * z_hi + 24, 48 * k : 48 * k + 48]
            blank = jnp.zeros((8, 32), jnp.float32)
            upper = jnp.concatenate([piece[:8], piece[8:16], blank], axis=1)
            lower = jnp.concatenate([piece[16:], piece[16:], blank], axis=1)
            packed = jnp.concatenate([upper, lower], axis=0)
            out_ref[8 * z_hi + k] = packed.astype(jnp.bfloat16)


def far_sum_kernel(parts_ref, out_ref):
    total = parts_ref[0].astype(jnp.float32)
    for k in range(1, 32):
        total += parts_ref[k].astype(jnp.float32)
    head = jnp.concatenate([total[:8, :48], total[:8, 48:96], total[8:, :48]], axis=0)
    out_ref[...] = head


def back_kernel(dir_ref, head_ref, out_ref):
    out_ref[...] = dot(dir_ref[...], head_ref[...], ((1,), (1,))).astype(jnp.bfloat16)


def column_order(core):
    new = jnp.arange(D, dtype=jnp.int32)
    side, x, z_hi, rest = new // 384, new // 96 % 4, new // 24 % 4, new % 24
    return z_hi * 192 + x * 48 + (side ^ core) * 24 + rest


def row_order():
    new = jnp.arange(D, dtype=jnp.int32)
    y_lo, z_lo, y_hi, rest = new // 384, new // 192 % 2, new // 48 % 4, new % 48
    return z_lo * 384 + (y_hi * 2 + y_lo) * 48 + rest


def order_matrix(old):
    return (old[:, None] == jnp.arange(D, dtype=jnp.int32)[None, :]).astype(jnp.bfloat16)


def on_device(
    image_feat, text_emb, head_weight, lang_ids, pair_mask, weight_codes, log_scale, logit_bias
):
    place = lax.axis_index("blk") % 8
    lang_count = pair_mask.shape[0]
    allowed = jnp.maximum(pair_mask, jnp.eye(lang_count, dtype=jnp.int32)).astype(jnp.float32)
    codes = weight_codes.astype(jnp.float32)
    table = (allowed * (0.25 * (codes[:, None] + codes[None, :]))).astype(jnp.bfloat16)
    extra = LABELS - lang_count
    table = jnp.pad(table, ((0, extra), (0, extra)))
    scale = jnp.exp(log_scale)
    text_scalars, image_scalars = [
        jnp.stack([scale, logit_bias] + [flag.astype(jnp.float32) for flag in flags])
        for flags in (
            [
                relay | inner, spot == 1, spot == 0, (spot % 2 == 1) & (spot != 1),
                (spot != 1) & ~inner, ~relay,
            ]
            for spot, relay, inner in [
                (spot, spot == 2, (spot == 4) | (spot == 6)) for spot in (place, 7 - place)
            ]
        )
    ]
    image_pick = jnp.where(place == 0, 2, jnp.where(place == 5, 1, 0)).reshape(1)
    langs = lang_ids.reshape(1, ROWS)
    block = array((ROWS + TAIL, D), jnp.bfloat16)
    total = array((ROWS, D), jnp.float32)
    scratch = [pltpu.VMEM(total.shape, total.dtype)]

    (text_out,) = call(text_kernel, 0.3, [block], (text_emb, langs))
    text_far = permute(text_out, lambda i: i + 2 if i % 8 != 7 else i - 6)
    text_mix = permute(
        text_out, lambda i: i + 1 if i % 2 == 0 else {5: i + 3, 7: i - 5}.get(i % 8)
    )

    image_out, image_inv = call(
        image_kernel,
        1.0,
        [block, array((ROWS, 1), jnp.float32)],
        (image_feat, head_weight, langs),
    )
    image_far = permute(image_out, lambda i: i - 2 if i % 8 != 0 else i + 6)
    image_mix = permute(
        image_out, lambda i: i - 1 if i % 2 == 1 else {2: i - 3, 0: i + 5}.get(i % 8)
    )

    own_hot = (lang_ids[:, None] == jnp.arange(LABELS)[None, :]).astype(jnp.bfloat16)
    image_rows = dot(own_hot, table).astype(jnp.bfloat16)
    text_rows = dot(own_hot, table, ((1,), (1,))).astype(jnp.bfloat16)
    feat_turned = dot(image_feat, order_matrix(row_order()), ((1,), (1,))).astype(jnp.bfloat16)
    feat_near = swap_cores(feat_turned)
    order = order_matrix(column_order(place % 2))
    (image_sum,) = call(
        own_kernel, 1.5, [total], (text_scalars, image_out, image_rows, text_out), 1
    )
    text_far, feat_near, image_sum, order = lax.optimization_barrier(
        (text_far, feat_near, image_sum, order)
    )

    text_hop = permute(text_far, lambda i: {1: i + 8, 3: i + 1, 5: i + 1}.get(i % 8))
    text_skip = permute(text_mix, lambda i: {2: i + 8}.get(i % 8))
    text_near = permute(text_far, lambda i: i ^ 1 if i % 8 != 1 else None)
    (image_sum,) = call(
        middle_kernel,
        2.6,
        [total],
        (text_scalars, image_out, image_rows, text_mix, text_far, image_sum),
        1,
    )
    image_pass = pick(image_pick, image_far, image_mix, image_out)
    text_hop, text_skip, image_sum, image_pass = lax.optimization_barrier(
        (text_hop, text_skip, image_sum, image_pass)
    )
    text_corner = permute(text_hop, lambda i: {1: i - 1}.get(i % 8))
    (image_sum,) = call(
        near_kernel,
        1.6,
        [total],
        (text_scalars, image_out, image_rows, text_near, image_sum),
        1,
    )
    half = array((HALF, ROWS), jnp.bfloat16)
    image_dir, keep, send = call(
        image_last_kernel,
        3.0,
        [array((ROWS, D), jnp.bfloat16), half, half],
        (
            text_scalars, image_out, image_rows, text_hop, text_skip, text_corner, image_sum,
            image_inv, order,
        ),
        1,
        scratch,
    )
    got = swap_cores(send)
    (image_back,) = call(
        back_kernel, 1.5, [array((ROWS, D), jnp.bfloat16)], (image_dir, head_weight)
    )
    got, image_back = lax.optimization_barrier((got, image_back))
    head = head_product(keep, got, feat_turned, feat_near)
    image_far, image_pass, head = lax.optimization_barrier((image_far, image_pass, head))
    image_late = permute(
        image_pass, lambda i: {6: i - 8, 5: i - 8, 4: i - 1, 2: i - 1, 0: i - 1}.get(i % 8)
    )
    image_near = permute(image_far, lambda i: i ^ 1 if i % 8 != 6 else None)
    head = exchange(head, NEAR_GROUPS)
    (head,) = call(
        near_sum_kernel,
        0.5,
        [array((32, 16, 128), jnp.bfloat16)],
        (head,),
    )
    text_out, head = lax.optimization_barrier((text_out, head))
    head = exchange(head, FAR_GROUPS)
    (head_grad,) = call(far_sum_kernel, 0.5, [array((24, 48), jnp.float32)], (head,))

    (text_sum,) = call(
        text_middle_kernel,
        5.0,
        [total],
        (image_scalars, text_out, text_rows, image_out, image_mix, image_far, image_near),
        1,
    )
    (text_back,) = call(
        text_last_kernel,
        3.0,
        [array((ROWS, D), jnp.bfloat16)],
        (image_scalars, text_out, text_rows, image_late, text_sum, text_emb),
        1,
        scratch,
    )
    return (image_back, text_back, head_grad.T)


def solution(mesh):
    in_specs = (
        P(("blk", "lane"), None),
        P(("blk", "lane"), None),
        P(),
        P(("blk", "lane")),
        P(),
        P(),
        P(),
        P(),
    )
    out_specs = (P(("blk", "lane"), None), P(("blk", "lane"), None), P("lane", "blk"))
    return jax.shard_map(
        on_device, mesh=mesh, in_specs=in_specs, out_specs=out_specs, check_vma=False
    )
```

```python
import jax
import jax.numpy as jnp
from jax import lax
from jax.experimental import pallas as pl
from jax.experimental.pallas import tpu as pltpu
from jax.sharding import PartitionSpec as P

D = 768
HALF = D // 2
ROWS = 384
TAIL = 16
LABELS = 128
N_BLK = 32
EPSILON = 1e-06
VMEM_BYTES = 20 * 1024 * 1024


def device_index(z_hi, x, core, z_lo, y):
    return ((z_hi * 4 + x) * 2 + core) * 16 + z_lo * 8 + y


NEAR_GROUPS = [
    [device_index(z_hi, x, core, z_lo, 2 * y_hi + y_lo) for x in range(4) for y_lo in range(2)]
    for z_hi in range(4)
    for core in range(2)
    for z_lo in range(2)
    for y_hi in range(4)
]
FAR_GROUPS = [
    [
        device_index(z_hi, x, core, z_lo, 2 * y_hi + y_lo)
        for z_hi in range(4)
        for z_lo in range(2)
        for y_hi in range(4)
    ]
    for x in range(4)
    for core in range(2)
    for y_lo in range(2)
]


def permute(value, target):
    pairs = [(i, target(i)) for i in range(N_BLK)]
    return lax.ppermute(value, "blk", [(i, j % N_BLK) for i, j in pairs if j is not None])


def swap_cores(value):
    return permute(value, lambda i: i ^ 1)


def exchange(value, groups):
    return lax.all_to_all(value, ("blk", "lane"), 0, 0, axis_index_groups=groups, tiled=True)


def dot(left, right, dims=((1,), (0,))):
    return lax.dot_general(left, right, (dims, ((), ())), preferred_element_type=jnp.float32)


def call(kernel, micros, outs, args, scalars=0, scratch=()):
    smem = pl.BlockSpec(memory_space=pltpu.SMEM)
    vmem = pl.BlockSpec(memory_space=pltpu.VMEM)
    return pl.pallas_call(
        kernel,
        out_shape=outs,
        in_specs=[smem] * scalars + [vmem] * (len(args) - scalars),
        out_specs=[vmem] * len(outs),
        scratch_shapes=scratch,
        cost_estimate=pl.CostEstimate(
            flops=int(micros * 1.1e9), bytes_accessed=int(micros * 3.0e6), transcendentals=0
        ),
        compiler_params=pltpu.CompilerParams(vmem_limit_bytes=VMEM_BYTES),
    )(*args)


def pick(index, first, second, third):
    anywhere = pl.BlockSpec(memory_space=pl.ANY)
    return pl.pallas_call(
        pick_kernel,
        out_shape=array(first.shape, first.dtype),
        in_specs=[pl.BlockSpec(memory_space=pltpu.SMEM)] + [anywhere] * 3,
        out_specs=pl.BlockSpec(memory_space=pltpu.VMEM),
        scratch_shapes=[pltpu.SemaphoreType.DMA(())],
        cost_estimate=pl.CostEstimate(flops=0, bytes_accessed=3000000, transcendentals=0),
    )(index, first, second, third)


def array(shape, dtype):
    return jax.ShapeDtypeStruct(shape, dtype)


def put_langs(langs_ref, out_ref):
    langs = langs_ref[...].reshape(1, ROWS).astype(jnp.float32)
    row = jnp.concatenate([langs, jnp.zeros((1, D - ROWS), jnp.float32)], axis=1)
    out_ref[ROWS:, :] = jnp.broadcast_to(row, (TAIL, D)).astype(jnp.bfloat16)


def text_kernel(text_ref, langs_ref, out_ref):
    text = text_ref[...].astype(jnp.float32)
    inverse = lax.rsqrt(jnp.sum(text * text, axis=-1, keepdims=True) + EPSILON)
    out_ref[:ROWS, :] = (text * inverse).astype(jnp.bfloat16)
    put_langs(langs_ref, out_ref)


def image_kernel(feat_ref, head_ref, langs_ref, out_ref, inv_ref):
    projected = dot(feat_ref[...], head_ref[...])
    inverse = lax.rsqrt(jnp.sum(projected * projected, axis=-1, keepdims=True) + EPSILON)
    inv_ref[...] = inverse
    out_ref[:ROWS, :] = (projected * inverse).astype(jnp.bfloat16)
    put_langs(langs_ref, out_ref)


def pair_term(scale, bias, own, own_rows, other_ref, positive):
    other = other_ref[:ROWS, :]
    langs = other_ref[ROWS : ROWS + 1, :ROWS].astype(jnp.int32)
    hot = lax.broadcasted_iota(jnp.int32, (LABELS, ROWS), 0) == langs
    weight = dot(own_rows, hot.astype(jnp.float32).astype(jnp.bfloat16))
    logit = scale * dot(own, other, ((1,), (1,))) + bias
    excess = 0.5 + 0.5 * jnp.tanh(0.5 * logit)
    if positive:
        row = lax.broadcasted_iota(jnp.int32, (ROWS, ROWS), 0)
        column = lax.broadcasted_iota(jnp.int32, (ROWS, ROWS), 1)
        excess = jnp.where(row == column, excess - 1.0, excess)
    return dot((weight * excess).astype(jnp.bfloat16), other)


def own_kernel(scalar_ref, own_ref, rows_ref, other_ref, sum_ref):
    sum_ref[...] = pair_term(
        scalar_ref[0], scalar_ref[1], own_ref[:ROWS, :], rows_ref[...], other_ref, True
    )


def add_term(scalar_ref, own_ref, rows_ref, other_ref, off, sum_ref):
    @pl.when(off == 0.0)
    def _():
        sum_ref[...] += pair_term(
            scalar_ref[0], scalar_ref[1], own_ref[:ROWS, :], rows_ref[...], other_ref, False
        )


def middle_kernel(scalar_ref, own_ref, rows_ref, same_ref, mix_ref, far_ref, sum_ref):
    own_kernel(scalar_ref, own_ref, rows_ref, same_ref, sum_ref)
    add_term(scalar_ref, own_ref, rows_ref, mix_ref, scalar_ref[2], sum_ref)
    add_term(scalar_ref, own_ref, rows_ref, far_ref, scalar_ref[3], sum_ref)


def near_kernel(scalar_ref, own_ref, rows_ref, near_ref, before_ref, sum_ref):
    sum_ref[...] = before_ref[...]
    add_term(scalar_ref, own_ref, rows_ref, near_ref, scalar_ref[4], sum_ref)


def pick_kernel(pick_ref, first_ref, second_ref, third_ref, out_ref, sem_ref):
    for index, ref in enumerate((first_ref, second_ref, third_ref)):

        @pl.when(pick_ref[0] == index)
        def _():
            copy = pltpu.make_async_copy(ref, out_ref, sem_ref)
            copy.start()
            copy.wait()


def image_last_kernel(
    scalar_ref, own_ref, rows_ref, hop_ref, skip_ref, corner_ref, before_ref, inv_ref, order_ref,
    dir_ref, keep_ref, send_ref, sum_ref,
):
    sum_ref[...] = before_ref[...]
    add_term(scalar_ref, own_ref, rows_ref, hop_ref, scalar_ref[6], sum_ref)
    add_term(scalar_ref, own_ref, rows_ref, skip_ref, scalar_ref[7], sum_ref)
    add_term(scalar_ref, own_ref, rows_ref, corner_ref, 1.0 - scalar_ref[4], sum_ref)
    grad = scalar_ref[0] * sum_ref[...]
    unit = own_ref[:ROWS, :].astype(jnp.float32)
    radial = jnp.sum(unit * grad, axis=-1, keepdims=True)
    direction = ((grad - unit * radial) * inv_ref[...]).astype(jnp.bfloat16)
    dir_ref[...] = direction
    turned = dot(order_ref[...], direction, ((1,), (1,))).astype(jnp.bfloat16)
    keep_ref[...] = turned[:HALF, :]
    send_ref[...] = turned[HALF:, :]


def pair_of_blocks(scalar_ref, own, rows, first_ref, second_ref, keeps, positive, both_ref):
    both_ref[:ROWS, :] = first_ref[:ROWS, :]
    both_ref[ROWS:, :] = second_ref[:ROWS, :]
    langs = [ref[ROWS : ROWS + 1, :ROWS].astype(jnp.int32) for ref in (first_ref, second_ref)]
    langs = jnp.concatenate(langs, axis=1)
    hot = lax.broadcasted_iota(jnp.int32, (LABELS, 2 * ROWS), 0) == langs
    weight = dot(rows, hot.astype(jnp.float32).astype(jnp.bfloat16))
    column = lax.broadcasted_iota(jnp.int32, (ROWS, 2 * ROWS), 1)
    weight = weight * jnp.where(column < ROWS, keeps[0], keeps[1])
    logit = scalar_ref[0] * dot(own, both_ref[...], ((1,), (1,))) + scalar_ref[1]
    excess = 0.5 + 0.5 * jnp.tanh(0.5 * logit)
    if positive:
        row = lax.broadcasted_iota(jnp.int32, (ROWS, 2 * ROWS), 0)
        excess = jnp.where(row == column, excess - 1.0, excess)
    return dot((weight * excess).astype(jnp.bfloat16), both_ref[...])


def text_middle_kernel(
    scalar_ref, own_ref, rows_ref, same_ref, mix_ref, far_ref, near_ref, sum_ref, both_ref
):
    own, rows = own_ref[:ROWS, :], rows_ref[...]
    keeps = (1.0, 1.0 - scalar_ref[2])
    sum_ref[...] = pair_of_blocks(
        scalar_ref, own, rows, same_ref, mix_ref, keeps, True, both_ref
    )
    keeps = (1.0 - scalar_ref[3], 1.0 - scalar_ref[4])
    sum_ref[...] += pair_of_blocks(
        scalar_ref, own, rows, far_ref, near_ref, keeps, False, both_ref
    )


def text_last_kernel(
    scalar_ref, text_ref, rows_ref, late_ref, before_ref, out_ref, sum_ref, own_ref
):
    text = text_ref[...].astype(jnp.float32)
    inverse = lax.rsqrt(jnp.sum(text * text, axis=-1, keepdims=True) + EPSILON)
    unit = text * inverse
    own_ref[...] = unit.astype(jnp.bfloat16)
    sum_ref[...] = before_ref[...]
    add_term(scalar_ref, own_ref, rows_ref, late_ref, scalar_ref[5], sum_ref)
    grad = scalar_ref[0] * sum_ref[...]
    radial = jnp.sum(unit * grad, axis=-1, keepdims=True)
    out_ref[...] = ((grad - unit * radial) * inverse).astype(jnp.bfloat16)


def head_kernel(keep_ref, got_ref, feat_ref, feat_near_ref, out_ref):
    head = dot(keep_ref[...], feat_ref[...]) + dot(got_ref[...], feat_near_ref[...])
    for x in range(4):
        out_ref[x, 0] = head[96 * x : 96 * x + 96, :].astype(jnp.bfloat16)


def head_product(keep, got, feat, feat_near):
    whole = pl.BlockSpec((HALF, ROWS), lambda y_lo: (0, 0))
    side = pl.BlockSpec((ROWS, HALF), lambda y_lo: (0, y_lo))
    head = pl.pallas_call(
        head_kernel,
        grid=(2,),
        out_shape=array((4, 2, 96, HALF), jnp.bfloat16),
        in_specs=[whole, whole, side, side],
        out_specs=pl.BlockSpec((4, 1, 96, HALF), lambda y_lo: (0, y_lo, 0, 0)),
        cost_estimate=pl.CostEstimate(
            flops=int(1.9e9), bytes_accessed=int(5.1e6), transcendentals=0
        ),
        compiler_params=pltpu.CompilerParams(vmem_limit_bytes=VMEM_BYTES),
    )(keep, got, feat, feat_near)
    return head.reshape(8, 96, HALF)


def near_sum_kernel(parts_ref, out_ref):
    total = parts_ref[0].astype(jnp.float32)
    for k in range(1, 8):
        total += parts_ref[k].astype(jnp.float32)
    for z_hi in range(4):
        for k in range(8):
            piece = total[24 * z_hi : 24 * z_hi + 24, 48 * k : 48 * k + 48]
            blank = jnp.zeros((8, 32), jnp.float32)
            upper = jnp.concatenate([piece[:8], piece[8:16], blank], axis=1)
            lower = jnp.concatenate([piece[16:], piece[16:], blank], axis=1)
            packed = jnp.concatenate([upper, lower], axis=0)
            out_ref[8 * z_hi + k] = packed.astype(jnp.bfloat16)


def far_sum_kernel(parts_ref, out_ref):
    total = parts_ref[0].astype(jnp.float32)
    for k in range(1, 32):
        total += parts_ref[k].astype(jnp.float32)
    head = jnp.concatenate([total[:8, :48], total[:8, 48:96], total[8:, :48]], axis=0)
    out_ref[...] = head


def back_kernel(dir_ref, head_ref, out_ref):
    out_ref[...] = dot(dir_ref[...], head_ref[...], ((1,), (1,))).astype(jnp.bfloat16)


def column_order(core):
    new = jnp.arange(D, dtype=jnp.int32)
    side, x, z_hi, rest = new // 384, new // 96 % 4, new // 24 % 4, new % 24
    return z_hi * 192 + x * 48 + (side ^ core) * 24 + rest


def row_order():
    new = jnp.arange(D, dtype=jnp.int32)
    y_lo, z_lo, y_hi, rest = new // 384, new // 192 % 2, new // 48 % 4, new % 48
    return z_lo * 384 + (y_hi * 2 + y_lo) * 48 + rest


def order_matrix(old):
    return (old[:, None] == jnp.arange(D, dtype=jnp.int32)[None, :]).astype(jnp.bfloat16)


def on_device(
    image_feat, text_emb, head_weight, lang_ids, pair_mask, weight_codes, log_scale, logit_bias
):
    place = lax.axis_index("blk") % 8
    lang_count = pair_mask.shape[0]
    allowed = jnp.maximum(pair_mask, jnp.eye(lang_count, dtype=jnp.int32)).astype(jnp.float32)
    codes = weight_codes.astype(jnp.float32)
    table = (allowed * (0.25 * (codes[:, None] + codes[None, :]))).astype(jnp.bfloat16)
    extra = LABELS - lang_count
    table = jnp.pad(table, ((0, extra), (0, extra)))
    scale = jnp.exp(log_scale)
    text_scalars, image_scalars = [
        jnp.stack([scale, logit_bias] + [flag.astype(jnp.float32) for flag in flags])
        for flags in (
            [
                relay | inner, spot == 1, spot == 0, (spot % 2 == 1) & (spot != 1),
                (spot != 1) & ~inner, ~relay,
            ]
            for spot, relay, inner in [
                (spot, spot == 2, (spot == 4) | (spot == 6)) for spot in (place, 7 - place)
            ]
        )
    ]
    image_pick = jnp.where(place == 0, 2, jnp.where(place == 5, 1, 0)).reshape(1)
    block = array((ROWS + TAIL, D), jnp.bfloat16)
    total = array((ROWS, D), jnp.float32)
    scratch = [pltpu.VMEM(total.shape, total.dtype)]

    (text_out,) = call(text_kernel, 0.3, [block], (text_emb, lang_ids))
    text_far = permute(text_out, lambda i: i + 2 if i % 8 != 7 else i - 6)
    text_mix = permute(
        text_out, lambda i: i + 1 if i % 2 == 0 else {5: i + 3, 7: i - 5}.get(i % 8)
    )

    image_out, image_inv = call(
        image_kernel,
        1.0,
        [block, array((ROWS, 1), jnp.float32)],
        (image_feat, head_weight, lang_ids),
    )
    image_far = permute(image_out, lambda i: i - 2 if i % 8 != 0 else i + 6)
    image_mix = permute(
        image_out, lambda i: i - 1 if i % 2 == 1 else {2: i - 3, 0: i + 5}.get(i % 8)
    )

    own_hot = (lang_ids[:, None] == jnp.arange(LABELS)[None, :]).astype(jnp.bfloat16)
    image_rows = dot(own_hot, table).astype(jnp.bfloat16)
    text_rows = dot(own_hot, table, ((1,), (1,))).astype(jnp.bfloat16)
    feat_turned = dot(image_feat, order_matrix(row_order()), ((1,), (1,))).astype(jnp.bfloat16)
    feat_near = swap_cores(feat_turned)
    order = order_matrix(column_order(place % 2))
    text_far, feat_near, order = lax.optimization_barrier((text_far, feat_near, order))

    text_hop = permute(text_far, lambda i: {1: i + 8, 3: i + 1, 5: i + 1}.get(i % 8))
    text_skip = permute(text_mix, lambda i: {2: i + 8}.get(i % 8))
    text_near = permute(text_far, lambda i: i ^ 1 if i % 8 != 1 else None)
    (image_sum,) = call(
        middle_kernel,
        3.6,
        [total],
        (text_scalars, image_out, image_rows, text_out, text_mix, text_far),
        1,
    )
    image_pass = pick(image_pick, image_far, image_mix, image_out)
    text_hop, text_skip, image_sum, image_pass = lax.optimization_barrier(
        (text_hop, text_skip, image_sum, image_pass)
    )
    text_corner = permute(text_hop, lambda i: {1: i - 1}.get(i % 8))
    (image_sum,) = call(
        near_kernel,
        1.6,
        [total],
        (text_scalars, image_out, image_rows, text_near, image_sum),
        1,
    )
    half = array((HALF, ROWS), jnp.bfloat16)
    image_dir, keep, send = call(
        image_last_kernel,
        3.0,
        [array((ROWS, D), jnp.bfloat16), half, half],
        (
            text_scalars, image_out, image_rows, text_hop, text_skip, text_corner, image_sum,
            image_inv, order,
        ),
        1,
        scratch,
    )
    got = swap_cores(send)
    (image_back,) = call(
        back_kernel, 1.5, [array((ROWS, D), jnp.bfloat16)], (image_dir, head_weight)
    )
    got, image_back = lax.optimization_barrier((got, image_back))
    head = head_product(keep, got, feat_turned, feat_near)
    image_far, image_pass, head = lax.optimization_barrier((image_far, image_pass, head))
    image_late = permute(
        image_pass, lambda i: {6: i - 8, 5: i - 8, 4: i - 1, 2: i - 1, 0: i - 1}.get(i % 8)
    )
    image_near = permute(image_far, lambda i: i ^ 1 if i % 8 != 6 else None)
    head = exchange(head, NEAR_GROUPS)
    (head,) = call(
        near_sum_kernel,
        0.5,
        [array((32, 16, 128), jnp.bfloat16)],
        (head,),
    )
    text_out, head = lax.optimization_barrier((text_out, head))
    head = exchange(head, FAR_GROUPS)
    (head_grad,) = call(far_sum_kernel, 0.5, [array((24, 48), jnp.float32)], (head,))

    (text_sum,) = call(
        text_middle_kernel,
        5.0,
        [total],
        (image_scalars, text_out, text_rows, image_out, image_mix, image_far, image_near),
        1,
        [pltpu.VMEM((2 * ROWS, D), jnp.bfloat16)],
    )
    (text_back,) = call(
        text_last_kernel,
        3.0,
        [array((ROWS, D), jnp.bfloat16)],
        (image_scalars, text_emb, text_rows, image_late, text_sum),
        1,
        scratch + [pltpu.VMEM((ROWS, D), jnp.bfloat16)],
    )
    return (image_back, text_back, head_grad.T)


def solution(mesh):
    in_specs = (
        P(("blk", "lane"), None),
        P(("blk", "lane"), None),
        P(),
        P(("blk", "lane")),
        P(),
        P(),
        P(),
        P(),
    )
    out_specs = (P(("blk", "lane"), None), P(("blk", "lane"), None), P("lane", "blk"))
    return jax.shard_map(
        on_device, mesh=mesh, in_specs=in_specs, out_specs=out_specs, check_vma=False
    )
```

```python
import jax
import jax.numpy as jnp
from jax import lax
from jax.experimental import pallas as pl
from jax.experimental.pallas import tpu as pltpu
from jax.sharding import PartitionSpec as P

D = 768
HALF = D // 2
ROWS = 384
TAIL = 16
LABELS = 128
N_BLK = 32
EPSILON = 1e-06
VMEM_BYTES = 20 * 1024 * 1024


def device_index(z_hi, x, core, z_lo, y):
    return ((z_hi * 4 + x) * 2 + core) * 16 + z_lo * 8 + y


NEAR_GROUPS = [
    [device_index(z_hi, x, core, z_lo, 2 * y_hi + y_lo) for x in range(4) for y_lo in range(2)]
    for z_hi in range(4)
    for core in range(2)
    for z_lo in range(2)
    for y_hi in range(4)
]
FAR_GROUPS = [
    [
        device_index(z_hi, x, core, z_lo, 2 * y_hi + y_lo)
        for z_hi in range(4)
        for z_lo in range(2)
        for y_hi in range(4)
    ]
    for x in range(4)
    for core in range(2)
    for y_lo in range(2)
]


def permute(value, target):
    pairs = [(i, target(i)) for i in range(N_BLK)]
    return lax.ppermute(value, "blk", [(i, j % N_BLK) for i, j in pairs if j is not None])


def swap_cores(value):
    return permute(value, lambda i: i ^ 1)


def exchange(value, groups):
    return lax.all_to_all(value, ("blk", "lane"), 0, 0, axis_index_groups=groups, tiled=True)


def dot(left, right, dims=((1,), (0,))):
    return lax.dot_general(left, right, (dims, ((), ())), preferred_element_type=jnp.float32)


def call(kernel, micros, outs, args, scalars=0, scratch=()):
    smem = pl.BlockSpec(memory_space=pltpu.SMEM)
    vmem = pl.BlockSpec(memory_space=pltpu.VMEM)
    return pl.pallas_call(
        kernel,
        out_shape=outs,
        in_specs=[smem] * scalars + [vmem] * (len(args) - scalars),
        out_specs=[vmem] * len(outs),
        scratch_shapes=scratch,
        cost_estimate=pl.CostEstimate(
            flops=int(micros * 1.1e9), bytes_accessed=int(micros * 3.0e6), transcendentals=0
        ),
        compiler_params=pltpu.CompilerParams(vmem_limit_bytes=VMEM_BYTES),
    )(*args)


def pick(index, first, second, third):
    anywhere = pl.BlockSpec(memory_space=pl.ANY)
    return pl.pallas_call(
        pick_kernel,
        out_shape=array(first.shape, first.dtype),
        in_specs=[pl.BlockSpec(memory_space=pltpu.SMEM)] + [anywhere] * 3,
        out_specs=pl.BlockSpec(memory_space=pltpu.VMEM),
        scratch_shapes=[pltpu.SemaphoreType.DMA(())],
        cost_estimate=pl.CostEstimate(flops=0, bytes_accessed=3000000, transcendentals=0),
    )(index, first, second, third)


def array(shape, dtype):
    return jax.ShapeDtypeStruct(shape, dtype)


def put_langs(langs_ref, out_ref):
    langs = langs_ref[...].reshape(1, ROWS).astype(jnp.float32)
    row = jnp.concatenate([langs, jnp.zeros((1, D - ROWS), jnp.float32)], axis=1)
    out_ref[ROWS:, :] = jnp.broadcast_to(row, (TAIL, D)).astype(jnp.bfloat16)


def text_kernel(text_ref, langs_ref, out_ref):
    text = text_ref[...].astype(jnp.float32)
    inverse = lax.rsqrt(jnp.sum(text * text, axis=-1, keepdims=True) + EPSILON)
    out_ref[:ROWS, :] = (text * inverse).astype(jnp.bfloat16)
    put_langs(langs_ref, out_ref)


def image_kernel(feat_ref, head_ref, langs_ref, out_ref, inv_ref):
    projected = dot(feat_ref[...], head_ref[...])
    inverse = lax.rsqrt(jnp.sum(projected * projected, axis=-1, keepdims=True) + EPSILON)
    inv_ref[...] = inverse
    out_ref[:ROWS, :] = (projected * inverse).astype(jnp.bfloat16)
    put_langs(langs_ref, out_ref)


def pair_term(scale, bias, own, own_rows, other_ref, positive):
    other = other_ref[:ROWS, :]
    langs = other_ref[ROWS : ROWS + 1, :ROWS].astype(jnp.int32)
    hot = lax.broadcasted_iota(jnp.int32, (LABELS, ROWS), 0) == langs
    weight = dot(own_rows, hot.astype(jnp.float32).astype(jnp.bfloat16))
    logit = scale * dot(own, other, ((1,), (1,))) + bias
    excess = 0.5 + 0.5 * jnp.tanh(0.5 * logit)
    if positive:
        row = lax.broadcasted_iota(jnp.int32, (ROWS, ROWS), 0)
        column = lax.broadcasted_iota(jnp.int32, (ROWS, ROWS), 1)
        excess = jnp.where(row == column, excess - 1.0, excess)
    return dot((weight * excess).astype(jnp.bfloat16), other)


def own_kernel(scalar_ref, own_ref, rows_ref, other_ref, sum_ref):
    sum_ref[...] = pair_term(
        scalar_ref[0], scalar_ref[1], own_ref[:ROWS, :], rows_ref[...], other_ref, True
    )


def add_term(scalar_ref, own_ref, rows_ref, other_ref, off, sum_ref):
    @pl.when(off == 0.0)
    def _():
        sum_ref[...] += pair_term(
            scalar_ref[0], scalar_ref[1], own_ref[:ROWS, :], rows_ref[...], other_ref, False
        )


def middle_kernel(scalar_ref, own_ref, rows_ref, same_ref, mix_ref, far_ref, sum_ref):
    own_kernel(scalar_ref, own_ref, rows_ref, same_ref, sum_ref)
    add_term(scalar_ref, own_ref, rows_ref, mix_ref, scalar_ref[2], sum_ref)
    add_term(scalar_ref, own_ref, rows_ref, far_ref, scalar_ref[3], sum_ref)


def pick_kernel(pick_ref, first_ref, second_ref, third_ref, out_ref, sem_ref):
    for index, ref in enumerate((first_ref, second_ref, third_ref)):

        @pl.when(pick_ref[0] == index)
        def _():
            copy = pltpu.make_async_copy(ref, out_ref, sem_ref)
            copy.start()
            copy.wait()


def image_last_kernel(
    scalar_ref, own_ref, rows_ref, hop_ref, skip_ref, corner_ref, near_ref, before_ref, inv_ref,
    order_ref, dir_ref, keep_ref, send_ref, sum_ref,
):
    sum_ref[...] = before_ref[...]
    add_term(scalar_ref, own_ref, rows_ref, near_ref, scalar_ref[4], sum_ref)
    add_term(scalar_ref, own_ref, rows_ref, hop_ref, scalar_ref[6], sum_ref)
    add_term(scalar_ref, own_ref, rows_ref, skip_ref, scalar_ref[7], sum_ref)
    add_term(scalar_ref, own_ref, rows_ref, corner_ref, 1.0 - scalar_ref[4], sum_ref)
    grad = scalar_ref[0] * sum_ref[...]
    unit = own_ref[:ROWS, :].astype(jnp.float32)
    radial = jnp.sum(unit * grad, axis=-1, keepdims=True)
    direction = ((grad - unit * radial) * inv_ref[...]).astype(jnp.bfloat16)
    dir_ref[...] = direction
    turned = dot(order_ref[...], direction, ((1,), (1,))).astype(jnp.bfloat16)
    keep_ref[...] = turned[:HALF, :]
    send_ref[...] = turned[HALF:, :]


def pair_of_blocks(scalar_ref, own, rows, first_ref, second_ref, keeps, positive, both_ref):
    both_ref[:ROWS, :] = first_ref[:ROWS, :]
    both_ref[ROWS:, :] = second_ref[:ROWS, :]
    langs = [ref[ROWS : ROWS + 1, :ROWS].astype(jnp.int32) for ref in (first_ref, second_ref)]
    langs = jnp.concatenate(langs, axis=1)
    hot = lax.broadcasted_iota(jnp.int32, (LABELS, 2 * ROWS), 0) == langs
    weight = dot(rows, hot.astype(jnp.float32).astype(jnp.bfloat16))
    column = lax.broadcasted_iota(jnp.int32, (ROWS, 2 * ROWS), 1)
    weight = weight * jnp.where(column < ROWS, keeps[0], keeps[1])
    logit = scalar_ref[0] * dot(own, both_ref[...], ((1,), (1,))) + scalar_ref[1]
    excess = 0.5 + 0.5 * jnp.tanh(0.5 * logit)
    if positive:
        row = lax.broadcasted_iota(jnp.int32, (ROWS, 2 * ROWS), 0)
        excess = jnp.where(row == column, excess - 1.0, excess)
    return dot((weight * excess).astype(jnp.bfloat16), both_ref[...])


def text_middle_kernel(
    scalar_ref, own_ref, rows_ref, same_ref, mix_ref, far_ref, near_ref, sum_ref, both_ref
):
    own, rows = own_ref[:ROWS, :], rows_ref[...]
    keeps = (1.0, 1.0 - scalar_ref[2])
    sum_ref[...] = pair_of_blocks(
        scalar_ref, own, rows, same_ref, mix_ref, keeps, True, both_ref
    )
    keeps = (1.0 - scalar_ref[3], 1.0 - scalar_ref[4])
    sum_ref[...] += pair_of_blocks(
        scalar_ref, own, rows, far_ref, near_ref, keeps, False, both_ref
    )


def text_last_kernel(
    scalar_ref, text_ref, rows_ref, late_ref, before_ref, out_ref, sum_ref, own_ref
):
    text = text_ref[...].astype(jnp.float32)
    inverse = lax.rsqrt(jnp.sum(text * text, axis=-1, keepdims=True) + EPSILON)
    unit = text * inverse
    own_ref[...] = unit.astype(jnp.bfloat16)
    sum_ref[...] = before_ref[...]
    add_term(scalar_ref, own_ref, rows_ref, late_ref, scalar_ref[5], sum_ref)
    grad = scalar_ref[0] * sum_ref[...]
    radial = jnp.sum(unit * grad, axis=-1, keepdims=True)
    out_ref[...] = ((grad - unit * radial) * inverse).astype(jnp.bfloat16)


def head_kernel(keep_ref, got_ref, feat_ref, feat_near_ref, out_ref):
    head = dot(keep_ref[...], feat_ref[...]) + dot(got_ref[...], feat_near_ref[...])
    for x in range(4):
        out_ref[x, 0] = head[96 * x : 96 * x + 96, :].astype(jnp.bfloat16)


def head_product(keep, got, feat, feat_near):
    whole = pl.BlockSpec((HALF, ROWS), lambda y_lo: (0, 0))
    side = pl.BlockSpec((ROWS, HALF), lambda y_lo: (0, y_lo))
    head = pl.pallas_call(
        head_kernel,
        grid=(2,),
        out_shape=array((4, 2, 96, HALF), jnp.bfloat16),
        in_specs=[whole, whole, side, side],
        out_specs=pl.BlockSpec((4, 1, 96, HALF), lambda y_lo: (0, y_lo, 0, 0)),
        cost_estimate=pl.CostEstimate(
            flops=int(1.9e9), bytes_accessed=int(5.1e6), transcendentals=0
        ),
        compiler_params=pltpu.CompilerParams(vmem_limit_bytes=VMEM_BYTES),
    )(keep, got, feat, feat_near)
    return head.reshape(8, 96, HALF)


def near_sum_kernel(parts_ref, out_ref):
    total = parts_ref[0].astype(jnp.float32)
    for k in range(1, 8):
        total += parts_ref[k].astype(jnp.float32)
    for z_hi in range(4):
        for k in range(8):
            piece = total[24 * z_hi : 24 * z_hi + 24, 48 * k : 48 * k + 48]
            blank = jnp.zeros((8, 32), jnp.float32)
            upper = jnp.concatenate([piece[:8], piece[8:16], blank], axis=1)
            lower = jnp.concatenate([piece[16:], piece[16:], blank], axis=1)
            packed = jnp.concatenate([upper, lower], axis=0)
            out_ref[8 * z_hi + k] = packed.astype(jnp.bfloat16)


def far_sum_kernel(parts_ref, out_ref):
    total = parts_ref[0].astype(jnp.float32)
    for k in range(1, 32):
        total += parts_ref[k].astype(jnp.float32)
    head = jnp.concatenate([total[:8, :48], total[:8, 48:96], total[8:, :48]], axis=0)
    out_ref[...] = head


def back_kernel(dir_ref, head_ref, out_ref):
    out_ref[...] = dot(dir_ref[...], head_ref[...], ((1,), (1,))).astype(jnp.bfloat16)


def column_order(core):
    new = jnp.arange(D, dtype=jnp.int32)
    side, x, z_hi, rest = new // 384, new // 96 % 4, new // 24 % 4, new % 24
    return z_hi * 192 + x * 48 + (side ^ core) * 24 + rest


def row_order():
    new = jnp.arange(D, dtype=jnp.int32)
    y_lo, z_lo, y_hi, rest = new // 384, new // 192 % 2, new // 48 % 4, new % 48
    return z_lo * 384 + (y_hi * 2 + y_lo) * 48 + rest


def order_matrix(old):
    return (old[:, None] == jnp.arange(D, dtype=jnp.int32)[None, :]).astype(jnp.bfloat16)


def on_device(
    image_feat, text_emb, head_weight, lang_ids, pair_mask, weight_codes, log_scale, logit_bias
):
    place = lax.axis_index("blk") % 8
    lang_count = pair_mask.shape[0]
    allowed = jnp.maximum(pair_mask, jnp.eye(lang_count, dtype=jnp.int32)).astype(jnp.float32)
    codes = weight_codes.astype(jnp.float32)
    table = (allowed * (0.25 * (codes[:, None] + codes[None, :]))).astype(jnp.bfloat16)
    extra = LABELS - lang_count
    table = jnp.pad(table, ((0, extra), (0, extra)))
    scale = jnp.exp(log_scale)
    text_scalars, image_scalars = [
        jnp.stack([scale, logit_bias] + [flag.astype(jnp.float32) for flag in flags])
        for flags in (
            [
                relay | inner, spot == 1, spot == 0, (spot % 2 == 1) & (spot != 1),
                (spot != 1) & ~inner, ~relay,
            ]
            for spot, relay, inner in [
                (spot, spot == 2, (spot == 4) | (spot == 6)) for spot in (place, 7 - place)
            ]
        )
    ]
    image_pick = jnp.where(place == 0, 2, jnp.where(place == 5, 1, 0)).reshape(1)
    block = array((ROWS + TAIL, D), jnp.bfloat16)
    total = array((ROWS, D), jnp.float32)
    scratch = [pltpu.VMEM(total.shape, total.dtype)]

    (text_out,) = call(text_kernel, 0.3, [block], (text_emb, lang_ids))
    text_far = permute(text_out, lambda i: i + 2 if i % 8 != 7 else i - 6)
    text_mix = permute(
        text_out, lambda i: i + 1 if i % 2 == 0 else {5: i + 3, 7: i - 5}.get(i % 8)
    )

    image_out, image_inv = call(
        image_kernel,
        1.0,
        [block, array((ROWS, 1), jnp.float32)],
        (image_feat, head_weight, lang_ids),
    )
    image_far = permute(image_out, lambda i: i - 2 if i % 8 != 0 else i + 6)
    image_mix = permute(
        image_out, lambda i: i - 1 if i % 2 == 1 else {2: i - 3, 0: i + 5}.get(i % 8)
    )

    own_hot = (lang_ids[:, None] == jnp.arange(LABELS)[None, :]).astype(jnp.bfloat16)
    image_rows = dot(own_hot, table).astype(jnp.bfloat16)
    text_rows = dot(own_hot, table, ((1,), (1,))).astype(jnp.bfloat16)
    feat_turned = dot(image_feat, order_matrix(row_order()), ((1,), (1,))).astype(jnp.bfloat16)
    feat_near = swap_cores(feat_turned)
    order = order_matrix(column_order(place % 2))
    text_far, feat_near, order = lax.optimization_barrier((text_far, feat_near, order))

    text_hop = permute(text_far, lambda i: {1: i + 8, 3: i + 1, 5: i + 1}.get(i % 8))
    text_skip = permute(text_mix, lambda i: {2: i + 8}.get(i % 8))
    text_near = permute(text_far, lambda i: i ^ 1 if i % 8 != 1 else None)
    (image_sum,) = call(
        middle_kernel,
        3.6,
        [total],
        (text_scalars, image_out, image_rows, text_out, text_mix, text_far),
        1,
    )
    image_pass = pick(image_pick, image_far, image_mix, image_out)
    text_hop, text_skip, image_sum, image_pass = lax.optimization_barrier(
        (text_hop, text_skip, image_sum, image_pass)
    )
    text_corner = permute(text_hop, lambda i: {1: i - 1}.get(i % 8))
    half = array((HALF, ROWS), jnp.bfloat16)
    image_dir, keep, send = call(
        image_last_kernel,
        3.0,
        [array((ROWS, D), jnp.bfloat16), half, half],
        (
            text_scalars, image_out, image_rows, text_hop, text_skip, text_corner, text_near,
            image_sum, image_inv, order,
        ),
        1,
        scratch,
    )
    got = swap_cores(send)
    (image_back,) = call(
        back_kernel, 1.5, [array((ROWS, D), jnp.bfloat16)], (image_dir, head_weight)
    )
    got, image_back = lax.optimization_barrier((got, image_back))
    head = head_product(keep, got, feat_turned, feat_near)
    image_far, image_pass, head = lax.optimization_barrier((image_far, image_pass, head))
    image_late = permute(
        image_pass, lambda i: {6: i - 8, 5: i - 8, 4: i - 1, 2: i - 1, 0: i - 1}.get(i % 8)
    )
    image_near = permute(image_far, lambda i: i ^ 1 if i % 8 != 6 else None)
    head = exchange(head, NEAR_GROUPS)
    (head,) = call(
        near_sum_kernel,
        0.5,
        [array((32, 16, 128), jnp.bfloat16)],
        (head,),
    )
    text_out, head = lax.optimization_barrier((text_out, head))
    head = exchange(head, FAR_GROUPS)
    (head_grad,) = call(far_sum_kernel, 0.5, [array((24, 48), jnp.float32)], (head,))

    (text_sum,) = call(
        text_middle_kernel,
        5.0,
        [total],
        (image_scalars, text_out, text_rows, image_out, image_mix, image_far, image_near),
        1,
        [pltpu.VMEM((2 * ROWS, D), jnp.bfloat16)],
    )
    (text_back,) = call(
        text_last_kernel,
        3.0,
        [array((ROWS, D), jnp.bfloat16)],
        (image_scalars, text_emb, text_rows, image_late, text_sum),
        1,
        scratch + [pltpu.VMEM((ROWS, D), jnp.bfloat16)],
    )
    return (image_back, text_back, head_grad.T)


def solution(mesh):
    in_specs = (
        P(("blk", "lane"), None),
        P(("blk", "lane"), None),
        P(),
        P(("blk", "lane")),
        P(),
        P(),
        P(),
        P(),
    )
    out_specs = (P(("blk", "lane"), None), P(("blk", "lane"), None), P("lane", "blk"))
    return jax.shard_map(
        on_device, mesh=mesh, in_specs=in_specs, out_specs=out_specs, check_vma=False
    )
```
